128 devices in a mesh: seq: 16 (over y, z), col: 8 (over x, core).
Axes of the slice: x: 4, y: 4, z: 4, core: 2. Of those that a mesh axis runs over, the one named last changes fastest.
Arguments:
- atom_feats: bfloat16 [16, 16384, 128], P(None, ('seq', 'col')), may hold values from -6 to 6
- atom_pair: bfloat16 [16, 512, 32, 128], P(None, ('seq', 'col'))
- key_shift: int32 [512], P(('seq', 'col')), may hold values from -1 to 1
- atom_token: int32 [16384], P(('seq', 'col')), may hold values from 0 to 2047, as said below
- token_count: int32 [2048], P('seq'), may hold values from 1 to 15, as said below
- atom_gain: float32 [128], replicated, may hold values from 0.5 to 1.5
- atom_qkv: bfloat16 [128, 384], replicated, may hold values from -0.5 to 0.5
- atom_out_proj: bfloat16 [128, 128], replicated, may hold values from -0.5 to 0.5
- atom_pair_proj: bfloat16 [16, 4], replicated
- pool_proj: bfloat16 [128, 768], replicated, may hold values from -0.5 to 0.5
- token_gain: float32 [768], replicated, may hold values from 0.5 to 1.5
- token_qkvg: bfloat16 [768, 4, 768], P(None, None, 'col'), may hold values from -0.21875 to 0.21875
- pair_tiles: bfloat16 [2048, 2048, 128], P('seq', 'col')
- pair_proj: bfloat16 [128, 16], replicated
- token_out_proj: bfloat16 [768, 768], replicated, may hold values from -0.21875 to 0.21875
- return_proj: bfloat16 [768, 128], replicated, may hold values from -0.21875 to 0.21875
Outputs:
- atom_update: bfloat16 [16, 16384, 128], P(None, ('seq', 'col'))
The draws below stay inside these ranges and needn't reach their ends.
Inputs may be any that keep to these rules, and one draw needn't show every extreme that they name: `token_count`: the tokens of one index of seq, 128 in a row, together own exactly 1024 atoms; the first token of each such block has the most atoms. `atom_token`: never falling; token t owns the token_count[t] atoms that follow those of earlier tokens.
All inputs are finite; a program needn't handle non-finite values.
Results may differ from the reference program's by a relative error of at most 0.015.
Values may be sent and summed in bfloat16 or wider, within the bound.
No kernel may reach another device: no remote copies, remote signals or barrier semaphores. Data moves between devices by JAX's collectives and lax.ppermute only.
A program may use at most 192 MiB of HBM per device.

```python
import jax
import jax.numpy as jnp
from jax import lax

C_ATOM = 128
ATOM_HEADS = 4
C_APAIR = 16
QBLOCK = 32
KWIN = 128
ATOM_MEAN = 8
C_TOKEN = 768
TOK_HEADS = 16
C_PAIR = 128
TOK_SEQ = 128
SAMPLES = 16
TOKENS = 2048
ATOMS = 16384
NBLK = 512


def token_layout(seed_key):
    block_count = TOKENS // TOK_SEQ
    shifts = jax.random.randint(seed_key, (block_count, TOK_SEQ), 0, ATOM_MEAN)
    shifts = shifts.at[:, 0].set(ATOM_MEAN - 1).at[:, 1].set(0).at[:, 2].set(ATOM_MEAN - 1)
    return ATOM_MEAN + shifts - jnp.roll(shifts, -1, axis=1)


def draw_atom_pair(key, part):
    key = jax.random.fold_in(key, 12)
    subkeys = jax.random.split(key, 1)
    field = jax.random.normal(subkeys[0], (C_APAIR, NBLK, QBLOCK, KWIN), jnp.float32)
    return field.astype(jnp.bfloat16)


def draw_atom_pair_proj(key, part):
    key = jax.random.fold_in(key, 11)
    matrix = jax.random.normal(key, (C_APAIR, ATOM_HEADS), jnp.float32) * C_APAIR ** (-0.5)
    return matrix.astype(jnp.bfloat16)


def draw_pair_tiles(key, part):
    key = jax.random.fold_in(key, 13)
    subkeys = jax.random.split(key, 1)
    field = jax.random.normal(subkeys[0], (TOKENS, TOKENS, C_PAIR), jnp.float32)
    return field.astype(jnp.bfloat16)


def draw_pair_proj(key, part):
    key = jax.random.fold_in(key, 14)
    matrix = jax.random.normal(key, (C_PAIR, TOK_HEADS), jnp.float32) * C_PAIR ** (-0.5)
    return matrix.astype(jnp.bfloat16)


def draw_token_count(key, part):
    counts = token_layout(key)
    return counts.reshape(-1).astype(jnp.int32)


def draw_atom_token(key, part):
    counts = token_layout(key)
    block_count = TOKENS // TOK_SEQ
    bounds = jnp.cumsum(counts, axis=1)
    positions = jnp.arange(ATOM_MEAN * TOK_SEQ, dtype=jnp.int32)
    local_tok = jnp.sum((bounds[:, None, :] <= positions[None, :, None]).astype(jnp.int32), axis=2)
    owners = local_tok + TOK_SEQ * jnp.arange(block_count, dtype=jnp.int32)[:, None]
    return owners.reshape(-1).astype(jnp.int32)


def set_ends(entries, rng, smallest, high):
    shape = entries.shape
    place = [jax.random.randint(jax.random.fold_in(rng, axis), (), 0, shape[axis]) for axis in range(len(shape))]
    entries = entries.at[tuple(place)].set(smallest)
    longest = shape.index(max(shape))
    place[longest] = (place[longest] + 1) % shape[longest]
    return entries.at[tuple(place)].set(high)


def block_scale(key, extent, cuts, low, high):
    loudness, own = 1.0, jax.random.fold_in(key, 6)
    for position, blocks in cuts:
        steps = jnp.exp(jax.random.uniform(jax.random.fold_in(own, position), (blocks,), jnp.float32, low / len(cuts), high / len(cuts)))
        loudness = loudness * jnp.repeat(steps, extent[position] // blocks).reshape([-1 if axis == position else 1 for axis in range(len(extent))])
    return loudness


def normal_values(rng, extent, scale, limit, pieces=(), held_as=jnp.bfloat16):
    entries = jax.random.normal(rng, extent, jnp.float32) * scale
    if len(pieces) > 0:
        entries = block_scale(rng, extent, pieces, -0.22, 0.18) * entries
    return jnp.clip(entries, min=-limit, max=limit).astype(held_as)


def setup_inputs(seed: int = 0) -> dict:
    key_of = jax.random.split(jax.random.key(seed), 17)
    atom_feats = normal_values(key_of[0], (SAMPLES, ATOMS, C_ATOM), 1.0, 6.0, ((1, 128),))
    atom_pair = draw_atom_pair(jax.random.fold_in(key_of[16], 71), 0)
    key_shift = set_ends(jax.random.randint(key_of[2], (NBLK,), -1, 2), jax.random.fold_in(key_of[2], 1), -1, 1).astype(jnp.int32)
    atom_token = draw_atom_token(jax.random.fold_in(key_of[16], 71), 0)
    token_count = draw_token_count(jax.random.fold_in(key_of[16], 71), 0)
    atom_gain = jnp.clip(1.0 + 0.1 * jax.random.normal(key_of[5], (C_ATOM,), jnp.float32), 0.5, 1.5)
    atom_qkv = normal_values(key_of[6], (C_ATOM, 3 * C_ATOM), C_ATOM ** -0.5, 0.5)
    atom_out_proj = normal_values(key_of[7], (C_ATOM, C_ATOM), C_ATOM ** -0.5, 0.5)
    atom_pair_proj = draw_atom_pair_proj(jax.random.fold_in(key_of[16], 71), 0)
    pool_proj = normal_values(key_of[9], (C_ATOM, C_TOKEN), C_ATOM ** -0.5, 0.5)
    token_gain = jnp.clip(1.0 + 0.1 * jax.random.normal(key_of[10], (C_TOKEN,), jnp.float32), 0.5, 1.5)
    token_qkvg = normal_values(key_of[11], (C_TOKEN, 4, C_TOKEN), C_TOKEN ** -0.5, 0.21875, ((2, 8),))
    pair_tiles = draw_pair_tiles(jax.random.fold_in(key_of[16], 71), 0)
    pair_proj = draw_pair_proj(jax.random.fold_in(key_of[16], 71), 0)
    token_out_proj = normal_values(key_of[14], (C_TOKEN, C_TOKEN), C_TOKEN ** -0.5, 0.21875)
    return_proj = normal_values(key_of[15], (C_TOKEN, C_ATOM), C_TOKEN ** -0.5, 0.21875)
    return dict(atom_feats=atom_feats, atom_pair=atom_pair, key_shift=key_shift, atom_token=atom_token, token_count=token_count, atom_gain=atom_gain, atom_qkv=atom_qkv, atom_out_proj=atom_out_proj, atom_pair_proj=atom_pair_proj, pool_proj=pool_proj, token_gain=token_gain, token_qkvg=token_qkvg, pair_tiles=pair_tiles, pair_proj=pair_proj, token_out_proj=token_out_proj, return_proj=return_proj)


EPSILON = 1e-05

def layer_norm(values, norm_gain):
    centred = values - lax.optimization_barrier(jnp.mean(values, axis=-1, keepdims=True))
    variance = lax.optimization_barrier(jnp.mean(centred * centred, axis=-1, keepdims=True))
    return centred * lax.rsqrt(variance + EPSILON) * norm_gain

def atom_attention(atom_feats, atom_pair, key_shift, atom_gain, atom_qkv, atom_out_proj, atom_pair_proj):
    samples, atom_len, channels = atom_feats.shape
    blocks, qblock, window = (atom_pair.shape[1], atom_pair.shape[2], atom_pair.shape[3])
    head_count = atom_pair_proj.shape[1]
    head_dim = channels // head_count
    margin = window // 2 - qblock // 2 + qblock
    normed = layer_norm(atom_feats.astype(jnp.float32), atom_gain).astype(jnp.bfloat16)
    projected = jnp.dot(normed, atom_qkv, preferred_element_type=jnp.float32).astype(jnp.bfloat16)
    queries = projected[..., :channels]
    pair_kv = jnp.stack([projected[..., channels:2 * channels], projected[..., 2 * channels:]])
    padded = jnp.pad(pair_kv, ((0, 0), (0, 0), (margin, margin), (0, 0)))
    starts = qblock * jnp.arange(blocks, dtype=jnp.int32) + qblock // 2 - window // 2 + qblock * key_shift + margin
    key_index = (starts[:, None] + jnp.arange(window, dtype=jnp.int32)[None, :]).astype(jnp.int32)
    windows = jnp.take(padded, key_index, axis=2)
    in_range = (key_index - margin >= 0) & (key_index - margin < atom_len)
    query_heads = queries.reshape(samples, blocks, qblock, head_count, head_dim).astype(jnp.float32)
    key_heads = windows[0].reshape(samples, blocks, window, head_count, head_dim).astype(jnp.float32)
    value_heads = windows[1].reshape(samples, blocks, window, head_count, head_dim).astype(jnp.float32)
    scores = jnp.einsum('snqhd,snkhd->snhqk', query_heads, key_heads) / jnp.sqrt(jnp.float32(head_dim))
    pair_bias = jnp.einsum('cnqk,ch->nhqk', atom_pair.astype(jnp.float32), atom_pair_proj.astype(jnp.float32))
    scores = scores + pair_bias[None]
    scores = jnp.where(in_range[None, :, None, None, :], scores, jnp.float32(-1000000000.0))
    weights = jax.nn.softmax(scores, axis=-1).astype(jnp.bfloat16)
    blended = jnp.einsum('snhqk,snkhd->snqhd', weights.astype(jnp.float32), value_heads)
    blended = blended.astype(jnp.bfloat16).reshape(samples, atom_len, channels)
    output = atom_feats.astype(jnp.float32) + jnp.dot(blended, atom_out_proj, preferred_element_type=jnp.float32)
    return output.astype(jnp.bfloat16)

def reference(atom_feats, atom_pair, key_shift, atom_token, token_count, atom_gain, atom_qkv, atom_out_proj, atom_pair_proj, pool_proj, token_gain, token_qkvg, pair_tiles, pair_proj, token_out_proj, return_proj):
    samples = atom_feats.shape[0]
    tok_total = token_count.shape[0]
    tok_width = token_qkvg.shape[0]
    head_count = pair_proj.shape[1]
    head_dim = tok_width // head_count
    atom_mid = atom_attention(atom_feats, atom_pair, key_shift, atom_gain, atom_qkv, atom_out_proj, atom_pair_proj)
    lifted = jax.nn.relu(jnp.dot(atom_mid, pool_proj, preferred_element_type=jnp.float32)).astype(jnp.bfloat16)

    def pool_sample(sample_rows):
        return jax.ops.segment_sum(sample_rows.astype(jnp.float32), atom_token, num_segments=tok_total)
    tok_sum = lax.map(pool_sample, lifted)
    token_single = tok_sum / token_count.astype(jnp.float32)[:, None]
    token_normed = layer_norm(token_single, token_gain).astype(jnp.bfloat16)
    projected = jnp.einsum('stc,cfh->stfh', token_normed.astype(jnp.float32), token_qkvg.astype(jnp.float32))
    projected = projected.astype(jnp.bfloat16)
    split_shape = (samples, tok_total, head_count, head_dim)
    query_vals = projected[:, :, 0].reshape(split_shape)
    key_vals = projected[:, :, 1].reshape(split_shape)
    values = projected[:, :, 2].reshape(split_shape)
    gate_vals = projected[:, :, 3].reshape(split_shape)
    pair_bias = jnp.dot(pair_tiles, pair_proj, preferred_element_type=jnp.float32).astype(jnp.bfloat16)
    pair_bias = jnp.transpose(pair_bias, (2, 0, 1))

    def attend(operands):
        query_one, key_one, value_one, gate_one = operands
        scores = jnp.einsum('qhd,khd->hqk', query_one.astype(jnp.float32), key_one.astype(jnp.float32))
        scores = scores / jnp.sqrt(jnp.float32(head_dim)) + pair_bias.astype(jnp.float32)
        weights = jax.nn.softmax(scores, axis=-1).astype(jnp.bfloat16)
        attended = jnp.einsum('hqk,khd->qhd', weights.astype(jnp.float32), value_one.astype(jnp.float32))
        gated = jax.nn.sigmoid(gate_one.astype(jnp.float32)) * attended
        return gated.astype(jnp.bfloat16).reshape(tok_total, tok_width)
    token_gated = lax.map(attend, (query_vals, key_vals, values, gate_vals))
    token_new = token_single + jnp.dot(token_gated, token_out_proj, preferred_element_type=jnp.float32)
    token_back = jnp.dot(token_new.astype(jnp.bfloat16), return_proj, preferred_element_type=jnp.float32)
    token_back = token_back.astype(jnp.bfloat16)
    spread = jnp.take(token_back, atom_token, axis=1)
    return (atom_mid.astype(jnp.float32) + spread.astype(jnp.float32)).astype(jnp.bfloat16)
```

```python
import functools

import jax
import jax.numpy as jnp
import numpy as np
from jax import lax
from jax.experimental import pallas as pl
from jax.experimental.pallas import tpu as pltpu
from jax.sharding import PartitionSpec as P

EPSILON = 1e-05
LOG2E = float(np.log2(np.e))
VMEM_LIMIT = 48 * 1024 * 1024
BF = jnp.bfloat16
F32 = jnp.float32


def params(grid_dims=1):
    return pltpu.CompilerParams(
        dimension_semantics=("arbitrary",) * grid_dims, vmem_limit_bytes=VMEM_LIMIT
    )


def layer_norm(values, norm_gain):
    centred = values - jnp.mean(values, axis=-1, keepdims=True)
    variance = jnp.mean(centred * centred, axis=-1, keepdims=True)
    return centred * lax.rsqrt(variance + EPSILON) * norm_gain


def dot(a, b, contract):
    return lax.dot_general(a, b, ((contract[0:1], contract[1:2]), ((), ())), preferred_element_type=F32)


def atom_kernel(
    shift_ref, off_ref, wpair_ref, feats_ref, before_ref, after_ref, pair_ref, gain_ref,
    qkv_ref, out_proj_ref, mid_ref, bias_ref, kv_ref, *, limit_atoms,
):
    samples, atoms, channels = feats_ref.shape
    margin = before_ref.shape[1]
    cpair, blocks, qblock, window = pair_ref.shape
    heads = wpair_ref.shape[1]
    head_dim = channels // heads
    rows = atoms + 2 * margin

    @pl.when(pl.program_id(0) == 0)
    def _():
        lane = lax.broadcasted_iota(jnp.int32, (qblock, window), 1)
        for b in range(blocks):
            tiles = [pair_ref[c, b].astype(F32) for c in range(cpair)]
            key = off_ref[0] - margin + qblock * (b + 1 + shift_ref[b]) + lane
            ok = (key >= 0) & (key < limit_atoms)
            for h in range(heads):
                acc = tiles[0] * wpair_ref[0, h]
                for c in range(1, cpair):
                    acc = acc + tiles[c] * wpair_ref[c, h]
                bias_ref[b, h * qblock : (h + 1) * qblock, :] = jnp.where(ok, acc * LOG2E, -1e9)

    feats = feats_ref[...]
    stacked = jnp.concatenate([before_ref[...], feats, after_ref[...]], axis=1)
    flat = stacked.reshape(samples * rows, channels).astype(F32)
    normed = layer_norm(flat, gain_ref[...]).astype(BF)
    projected = jnp.dot(normed, qkv_ref[...], preferred_element_type=F32)
    kv_ref[...] = projected[:, channels:].astype(BF).reshape(samples, rows, 2 * channels)
    scale = LOG2E / float(np.sqrt(head_dim))
    queries = (projected[:, :channels] * scale).astype(BF).reshape(samples, rows, channels)
    lane_head = lax.broadcasted_iota(jnp.int32, (qblock, channels), 1) // head_dim
    masks = [lane_head == h for h in range(heads)]
    ones = jnp.ones((window, channels), BF)
    zero = jnp.zeros((qblock, channels), BF)
    attended = []
    for s in range(samples):
        for b in range(blocks):
            begin = pl.multiple_of(qblock * (b + 1 + shift_ref[b]), qblock)
            win = kv_ref[s, pl.ds(begin, window), :]
            q = queries[s, margin + b * qblock : margin + (b + 1) * qblock, :]
            spread = jnp.concatenate([jnp.where(m, q, zero) for m in masks], axis=0)
            scores = dot(spread, win[:, :channels], (1, 1)) + bias_ref[b]
            top = jnp.max(scores, axis=1, keepdims=True)
            weights = jnp.exp2(scores - top).astype(BF)
            both = jnp.concatenate([win[:, channels:], ones], axis=1)
            mixed = jnp.dot(weights, both, preferred_element_type=F32)
            mixed = mixed[:, :channels] / mixed[:, channels:]
            out = jnp.zeros((qblock, channels), F32)
            for h in range(heads):
                out = jnp.where(masks[h], mixed[h * qblock : (h + 1) * qblock], out)
            attended.append(out.astype(BF))
    attended = jnp.concatenate(attended, axis=0)
    update = jnp.dot(attended, out_proj_ref[...], preferred_element_type=F32)
    mid = feats.reshape(samples * atoms, channels).astype(F32) + update
    mid_ref[...] = mid.astype(BF).reshape(samples, atoms, channels)


def atom_attention(feats, before, after, pair, shift, offset, limit, gain, qkv, out_proj, wpair):
    samples, atoms, channels = feats.shape
    margin = before.shape[1]
    step = 4
    rows = atoms + 2 * margin
    blocks = pair.shape[1]
    whole = lambda a: pl.BlockSpec(a.shape, lambda i: (0,) * a.ndim)
    part = lambda a: pl.BlockSpec((step,) + a.shape[1:], lambda i: (i, 0, 0))
    smem = pl.BlockSpec(memory_space=pltpu.SMEM)
    return pl.pallas_call(
        functools.partial(atom_kernel, limit_atoms=limit),
        grid=(samples // step,),
        in_specs=[smem, smem, smem, part(feats), part(before), part(after), whole(pair),
                  whole(gain), whole(qkv), whole(out_proj)],
        out_specs=part(feats),
        out_shape=jax.ShapeDtypeStruct(feats.shape, BF),
        scratch_shapes=[
            pltpu.VMEM((blocks, pair.shape[2] * wpair.shape[1], pair.shape[3]), F32),
            pltpu.VMEM((step, rows, 2 * channels), BF),
        ],
        compiler_params=params(),
        cost_estimate=pl.CostEstimate(flops=8_000_000_000, bytes_accessed=3_000_000, transcendentals=1_000_000),
        name="atom_attention",
    )(shift, offset, wpair, feats, before, after, pair, gain, qkv, out_proj)


def token_kernel(
    mid_ref, count_row_ref, count_col_ref, pool_ref, gain_ref, w_ref, qkv_ref, gate_ref,
    single_ref, normed_ref, *, head_dim,
):
    peers, samples, atoms, channels = mid_ref.shape
    toks = count_col_ref.shape[0]
    total = peers * atoms

    @pl.when(pl.program_id(0) == 0)
    def _():
        counts = count_col_ref[...]
        row = lax.broadcasted_iota(jnp.int32, (toks, toks), 0)
        col = lax.broadcasted_iota(jnp.int32, (toks, toks), 1)
        spread = jnp.broadcast_to(count_row_ref[...], (toks, toks))
        ends = jnp.sum(jnp.where(col <= row, spread, 0.0), axis=1, keepdims=True)
        begins = ends - counts
        atom = lax.broadcasted_iota(jnp.int32, (toks, total), 1).astype(F32)
        onehot = jnp.where((atom >= begins) & (atom < ends), 1.0, 0.0).astype(BF)
        for s in range(samples):
            mid = mid_ref[:, s].reshape(total, channels)
            lifted = jnp.dot(mid, pool_ref[...], preferred_element_type=F32)
            lifted = jnp.maximum(lifted, 0.0).astype(BF)
            single = jnp.dot(onehot, lifted, preferred_element_type=F32) / counts
            single_ref[s] = single
            normed_ref[s * toks : (s + 1) * toks, :] = layer_norm(single, gain_ref[...]).astype(BF)

    projected = jnp.dot(normed_ref[...], w_ref[0], preferred_element_type=F32)
    turned = projected.T
    scale = LOG2E / float(np.sqrt(head_dim))
    width = turned.shape[0] // 4
    for hh in range(width // head_dim):
        for s in range(samples):
            for f in range(4):
                lo = f * width + hh * head_dim
                tile = turned[lo : lo + head_dim, s * toks : (s + 1) * toks]
                if f == 0:
                    tile = tile * scale
                if f < 3:
                    qkv_ref[hh, s, f] = tile.astype(BF)
                else:
                    gate_ref[hh, s] = tile.astype(BF)


def pool_and_project(mid, count, pool, gain, w, heads):
    peers, samples, atoms, channels = mid.shape
    toks = count.shape[0]
    width = pool.shape[1]
    head_dim = width // heads
    local = heads // peers
    count = count.astype(F32)
    whole = lambda a: pl.BlockSpec(a.shape, lambda i: (0,) * a.ndim)
    row, col = count.reshape(1, toks), count.reshape(toks, 1)
    gain = gain.reshape(1, width)
    return pl.pallas_call(
        functools.partial(token_kernel, head_dim=head_dim),
        grid=(peers,),
        in_specs=[whole(mid), whole(row), whole(col), whole(pool), whole(gain),
                  pl.BlockSpec((1,) + w.shape[1:], lambda i: (i, 0, 0))],
        out_specs=[
            pl.BlockSpec((local, samples, 3, head_dim, toks), lambda i: (i, 0, 0, 0, 0)),
            pl.BlockSpec((local, samples, head_dim, toks), lambda i: (i, 0, 0, 0)),
            pl.BlockSpec((samples, toks, width), lambda i: (0, 0, 0)),
        ],
        out_shape=[
            jax.ShapeDtypeStruct((heads, samples, 3, head_dim, toks), BF),
            jax.ShapeDtypeStruct((heads, samples, head_dim, toks), BF),
            jax.ShapeDtypeStruct((samples, toks, width), F32),
        ],
        scratch_shapes=[pltpu.VMEM((samples * toks, width), BF)],
        compiler_params=params(),
        cost_estimate=pl.CostEstimate(flops=6_000_000_000, bytes_accessed=8_000_000, transcendentals=1000),
        name="pool_and_project",
    )(mid, row, col, pool, gain, w)


def attend_kernel(qkv_ref, bias_ref, out_ref, keys_ref, values_ref, *, first):
    peers, samples, _, head_dim, toks = qkv_ref.shape
    qblocks = out_ref.shape[0]
    step = pl.program_id(0)

    @pl.when(step == 0)
    def _():
        for s in range(samples):
            for p in range(peers):
                keys_ref[s, :, p * toks : (p + 1) * toks] = qkv_ref[p, s, 1]
                values_ref[s, :head_dim, p * toks : (p + 1) * toks] = qkv_ref[p, s, 2]
            pad = values_ref.shape[1] - head_dim
            values_ref[s, head_dim:, :] = jnp.ones((pad, peers * toks), BF)

    bias = jnp.concatenate([bias_ref[c] for c in range(bias_ref.shape[0])], axis=1).astype(F32)
    for s in range(samples):
        queries = jnp.concatenate(
            [qkv_ref[first + step * qblocks + j, s, 0] for j in range(qblocks)], axis=1
        )
        scores = dot(queries, keys_ref[s], (0, 0)) + bias
        top = jnp.max(scores, axis=1, keepdims=True)
        weights = jnp.exp2(scores - top).astype(BF)
        mixed = dot(weights, values_ref[s], (1, 1))
        mixed = mixed / mixed[:, head_dim : head_dim + 1]
        turned = mixed.T
        for j in range(qblocks):
            out_ref[j, s] = turned[:head_dim, j * toks : (j + 1) * toks].astype(BF)


def token_attention(qkv, bias, first):
    peers, samples, _, head_dim, toks = qkv.shape
    cols, rows, width = bias.shape
    qblocks = 2
    tile = qblocks * toks
    keys = peers * toks
    return pl.pallas_call(
        functools.partial(attend_kernel, first=first),
        grid=(rows // tile,),
        in_specs=[
            pl.BlockSpec(qkv.shape, lambda i: (0, 0, 0, 0, 0)),
            pl.BlockSpec((cols, tile, width), lambda i: (0, i, 0)),
        ],
        out_specs=pl.BlockSpec((qblocks, samples, head_dim, toks), lambda i: (i, 0, 0, 0)),
        out_shape=jax.ShapeDtypeStruct((rows // toks, samples, head_dim, toks), BF),
        scratch_shapes=[
            pltpu.VMEM((samples, head_dim, keys), BF),
            pltpu.VMEM((samples, head_dim + 16, keys), BF),
        ],
        compiler_params=params(),
        cost_estimate=pl.CostEstimate(
            flops=4 * samples * rows * keys * 128, bytes_accessed=2 * rows * keys + 2 * qkv.size,
            transcendentals=samples * rows * keys,
        ),
        name="token_attention",
    )(qkv, bias)


def out_kernel(mixed_ref, gate_ref, single_ref, out_proj_ref, return_ref, back_ref):
    heads, samples, head_dim, toks = mixed_ref.shape
    for s in range(samples):
        gate = jax.nn.sigmoid(gate_ref[:, s].astype(F32))
        gated = (gate * mixed_ref[:, s].astype(F32)).astype(BF).reshape(heads * head_dim, toks)
        new = single_ref[s] + dot(gated, out_proj_ref[...], (0, 0))
        back_ref[s] = jnp.dot(new.astype(BF), return_ref[...], preferred_element_type=F32).astype(BF)


def out_project(mixed, gate, single, out_proj, return_proj):
    return pl.pallas_call(
        out_kernel,
        out_shape=jax.ShapeDtypeStruct(single.shape[:2] + return_proj.shape[1:], BF),
        compiler_params=pltpu.CompilerParams(vmem_limit_bytes=VMEM_LIMIT),
        cost_estimate=pl.CostEstimate(flops=400_000_000, bytes_accessed=4_000_000, transcendentals=200_000),
        name="out_project",
    )(mixed, gate, single, out_proj, return_proj)


def spread_kernel(tok_ref, back_ref, mid_ref, out_ref):
    samples, atoms, channels = mid_ref.shape
    toks = back_ref.shape[1]
    col = lax.broadcasted_iota(jnp.int32, (atoms, toks), 1)
    onehot = jnp.where(col == tok_ref[...], 1.0, 0.0).astype(BF)
    for s in range(samples):
        spread = jnp.dot(onehot, back_ref[s], preferred_element_type=F32)
        out_ref[s] = (mid_ref[s].astype(F32) + spread).astype(BF)


def spread_back(local_tok, back, mid):
    return pl.pallas_call(
        spread_kernel,
        out_shape=jax.ShapeDtypeStruct(mid.shape, BF),
        compiler_params=pltpu.CompilerParams(vmem_limit_bytes=VMEM_LIMIT),
        cost_estimate=pl.CostEstimate(flops=100_000_000, bytes_accessed=2_000_000, transcendentals=0),
        name="spread_back",
    )(local_tok, back, mid)


def shards(
    atom_feats, atom_pair, key_shift, atom_token, token_count, atom_gain, atom_qkv,
    atom_out_proj, atom_pair_proj, pool_proj, token_gain, token_qkvg, pair_tiles, pair_proj,
    token_out_proj, return_proj,
):
    samples, atoms, channels = atom_feats.shape
    toks = token_count.shape[0]
    width = token_qkvg.shape[0]
    heads = pair_proj.shape[1]
    peers = lax.axis_size("col")
    seqs = lax.axis_size("seq")
    devices = peers * seqs
    qblock, window = atom_pair.shape[2:]
    margin = window // 2 - qblock // 2 + qblock

    up = [(i, i + 1) for i in range(devices - 1)]
    down = [(j, i) for i, j in up]
    before = lax.ppermute(atom_feats[:, atoms - margin :], ("seq", "col"), up)
    after = lax.ppermute(atom_feats[:, :margin], ("seq", "col"), down)

    local_w = token_qkvg.reshape(width, -1)
    all_w = lax.all_gather(local_w, "col", axis=0)

    tile_bias = jnp.einsum("ijc,ch->hij", pair_tiles, pair_proj, preferred_element_type=F32)
    tile_bias = (tile_bias * LOG2E).astype(BF)
    head_bias = lax.all_to_all(tile_bias, "seq", split_axis=0, concat_axis=0, tiled=True)
    head_bias = head_bias.reshape(seqs * toks, -1)
    chunks = 2
    chunk = seqs * toks // chunks
    biases = [
        lax.all_gather(head_bias[i * chunk : (i + 1) * chunk], "col", axis=0) for i in range(chunks)
    ]

    index = lax.axis_index(("seq", "col"))
    offset = (index * atoms).astype(jnp.int32).reshape(1)
    mid = atom_attention(
        atom_feats, before, after, atom_pair, key_shift, offset, atoms * devices,
        atom_gain.reshape(1, -1), atom_qkv, atom_out_proj, atom_pair_proj.astype(F32),
    )
    mine = lax.all_to_all(
        mid.reshape(peers, samples // peers, atoms, channels), "col", split_axis=0, concat_axis=0, tiled=True
    )
    qkv, gate, single = pool_and_project(mine, token_count, pool_proj, token_gain, all_w, heads)
    qkv = lax.all_to_all(qkv, "seq", split_axis=0, concat_axis=0, tiled=True)
    mixed = jnp.concatenate(
        [token_attention(qkv, biases[i], i * (seqs // chunks)) for i in range(chunks)], axis=0
    )
    mixed = lax.all_to_all(mixed, "seq", split_axis=0, concat_axis=0, tiled=True)
    back = out_project(mixed, gate, single, token_out_proj, return_proj)
    back = lax.all_gather(back, "col", axis=0, tiled=True)
    local_tok = (atom_token - lax.axis_index("seq") * toks).reshape(atoms, 1)
    return spread_back(local_tok, back, mid)


def solution(mesh):
    placed = (
        P(None, ("seq", "col"), None),
        P(None, ("seq", "col"), None, None),
        P(("seq", "col")),
        P(("seq", "col")),
        P("seq"),
        P(),
        P(),
        P(),
        P(),
        P(),
        P(),
        P(None, None, "col"),
        P("seq", "col", None),
        P(),
        P(),
        P(),
    )
    return jax.shard_map(
        shards, mesh=mesh, in_specs=placed, out_specs=P(None, ("seq", "col"), None), check_vma=False
    )
```

```python
import functools

import jax
import jax.numpy as jnp
import numpy as np
from jax import lax
from jax.experimental import pallas as pl
from jax.experimental.pallas import tpu as pltpu
from jax.sharding import PartitionSpec as P

EPSILON = 1e-05
LOG2E = float(np.log2(np.e))
VMEM_LIMIT = 48 * 1024 * 1024
BF = jnp.bfloat16
F32 = jnp.float32


def params(limit=VMEM_LIMIT):
    return pltpu.CompilerParams(dimension_semantics=("arbitrary",), vmem_limit_bytes=limit)


def layer_norm(values, norm_gain):
    centred = values - jnp.mean(values, axis=-1, keepdims=True)
    variance = jnp.mean(centred * centred, axis=-1, keepdims=True)
    return centred * lax.rsqrt(variance + EPSILON) * norm_gain


def dot(a, b, contract):
    return lax.dot_general(a, b, ((contract[0:1], contract[1:2]), ((), ())), preferred_element_type=F32)


def atom_kernel(
    shift_ref, off_ref, wpair_ref, feats_ref, before_ref, after_ref, pair_ref, gain_ref,
    qkv_ref, out_proj_ref, mid_ref, bias_ref, kv_ref, *, limit_atoms,
):
    samples, atoms, channels = feats_ref.shape
    cpair, blocks, qblock, window = pair_ref.shape
    margin = window // 2 - qblock // 2 + qblock
    heads = wpair_ref.shape[1]
    head_dim = channels // heads
    rows = atoms + 2 * margin

    @pl.when(pl.program_id(0) == 0)
    def _():
        lane = lax.broadcasted_iota(jnp.int32, (qblock, window), 1)
        for b in range(blocks):
            tiles = [pair_ref[c, b].astype(F32) for c in range(cpair)]
            key = off_ref[0] - margin + qblock * (b + 1 + shift_ref[b]) + lane
            ok = (key >= 0) & (key < limit_atoms)
            for h in range(heads):
                acc = tiles[0] * wpair_ref[0, h]
                for c in range(1, cpair):
                    acc = acc + tiles[c] * wpair_ref[c, h]
                bias_ref[b, h * qblock : (h + 1) * qblock, :] = jnp.where(ok, acc * LOG2E, -1e9)

    feats = feats_ref[...]
    stacked = jnp.concatenate(
        [before_ref[:, atoms - margin :], feats, after_ref[:, :margin]], axis=1
    )
    flat = stacked.reshape(samples * rows, channels).astype(F32)
    normed = layer_norm(flat, gain_ref[...]).astype(BF)
    projected = jnp.dot(normed, qkv_ref[...], preferred_element_type=F32)
    kv_ref[...] = projected[:, channels:].astype(BF).reshape(samples, rows, 2 * channels)
    scale = LOG2E / float(np.sqrt(head_dim))
    queries = (projected[:, :channels] * scale).astype(BF).reshape(samples, rows, channels)
    lane_head = lax.broadcasted_iota(jnp.int32, (qblock, channels), 1) // head_dim
    masks = [lane_head == h for h in range(heads)]
    ones = jnp.ones((window, channels), BF)
    zero = jnp.zeros((qblock, channels), BF)
    attended = []
    for s in range(samples):
        for b in range(blocks):
            begin = pl.multiple_of(qblock * (b + 1 + shift_ref[b]), qblock)
            win = kv_ref[s, pl.ds(begin, window), :]
            q = queries[s, margin + b * qblock : margin + (b + 1) * qblock, :]
            spread = jnp.concatenate([jnp.where(m, q, zero) for m in masks], axis=0)
            scores = dot(spread, win[:, :channels], (1, 1)) + bias_ref[b]
            top = jnp.max(scores, axis=1, keepdims=True)
            weights = jnp.exp2(scores - top).astype(BF)
            both = jnp.concatenate([win[:, channels:], ones], axis=1)
            mixed = jnp.dot(weights, both, preferred_element_type=F32)
            mixed = mixed[:, :channels] / mixed[:, channels:]
            out = jnp.zeros((qblock, channels), F32)
            for h in range(heads):
                out = jnp.where(masks[h], mixed[h * qblock : (h + 1) * qblock], out)
            attended.append(out.astype(BF))
    attended = jnp.concatenate(attended, axis=0)
    update = jnp.dot(attended, out_proj_ref[...], preferred_element_type=F32)
    mid = feats.reshape(samples * atoms, channels).astype(F32) + update
    mid_ref[...] = mid.astype(BF).reshape(samples, atoms, channels)


def atom_attention(feats, before, after, pair, shift, offset, limit, gain, qkv, out_proj, wpair):
    samples, atoms, channels = feats.shape
    blocks, qblock, window = pair.shape[1:]
    rows = atoms + 2 * (window // 2 - qblock // 2 + qblock)
    step = 4
    whole = lambda a: pl.BlockSpec(a.shape, lambda i: (0,) * a.ndim)
    part = lambda a: pl.BlockSpec((step,) + a.shape[1:], lambda i: (i, 0, 0))
    smem = pl.BlockSpec(memory_space=pltpu.SMEM)
    return pl.pallas_call(
        functools.partial(atom_kernel, limit_atoms=limit),
        grid=(samples // step,),
        in_specs=[smem, smem, smem, part(feats), part(before), part(after), whole(pair),
                  whole(gain), whole(qkv), whole(out_proj)],
        out_specs=part(feats),
        out_shape=jax.ShapeDtypeStruct(feats.shape, BF),
        scratch_shapes=[
            pltpu.VMEM((blocks, qblock * wpair.shape[1], window), F32),
            pltpu.VMEM((step, rows, 2 * channels), BF),
        ],
        compiler_params=params(),
        cost_estimate=pl.CostEstimate(flops=8_000_000_000, bytes_accessed=3_000_000, transcendentals=1_000_000),
        name="atom_attention",
    )(shift, offset, wpair, feats, before, after, pair, gain, qkv, out_proj)


def tie(value, *others):
    def kernel(*refs):
        pass
    hbm = pl.BlockSpec(memory_space=pl.ANY)
    return pl.pallas_call(
        kernel,
        in_specs=[hbm] * (1 + len(others)),
        out_specs=hbm,
        out_shape=jax.ShapeDtypeStruct(value.shape, value.dtype),
        input_output_aliases={0: 0},
        name="tie",
    )(value, *others)


def token_kernel(
    mid_ref, count_row_ref, count_col_ref, pool_ref, gain_ref, w_ref, *refs, head_dim,
):
    qkv_ref, gate_ref, single_ref, normed_ref = refs[-4:]
    peers, samples, atoms, channels = mid_ref.shape
    toks = count_col_ref.shape[0]
    total = peers * atoms

    @pl.when(pl.program_id(0) == 0)
    def _():
        counts = count_col_ref[...]
        row = lax.broadcasted_iota(jnp.int32, (toks, toks), 0)
        col = lax.broadcasted_iota(jnp.int32, (toks, toks), 1)
        spread = jnp.broadcast_to(count_row_ref[...], (toks, toks))
        ends = jnp.sum(jnp.where(col <= row, spread, 0.0), axis=1, keepdims=True)
        begins = ends - counts
        atom = lax.broadcasted_iota(jnp.int32, (toks, total), 1).astype(F32)
        onehot = jnp.where((atom >= begins) & (atom < ends), 1.0, 0.0).astype(BF)
        for s in range(samples):
            mid = mid_ref[:, s].reshape(total, channels)
            lifted = jnp.dot(mid, pool_ref[...], preferred_element_type=F32)
            lifted = jnp.maximum(lifted, 0.0).astype(BF)
            single = jnp.dot(onehot, lifted, preferred_element_type=F32) / counts
            single_ref[s] = single
            normed_ref[s * toks : (s + 1) * toks, :] = layer_norm(single, gain_ref[...]).astype(BF)

    turned = dot(w_ref[0], normed_ref[...], (1, 1))
    scale = LOG2E / float(np.sqrt(head_dim))
    width = turned.shape[0] // 4
    for hh in range(width // head_dim):
        for s in range(samples):
            for f in range(4):
                lo = f * width + hh * head_dim
                tile = turned[lo : lo + head_dim, s * toks : (s + 1) * toks]
                if f == 0:
                    tile = tile * scale
                if f < 3:
                    qkv_ref[hh, s, f] = tile.astype(BF)
                else:
                    gate_ref[hh, s] = tile.astype(BF)


def pool_and_project(mid, count, pool, gain, w, heads, after):
    peers, samples, atoms, channels = mid.shape
    toks = count.shape[0]
    width = pool.shape[1]
    head_dim = width // heads
    local = heads // peers
    count = count.astype(F32)
    whole = lambda a: pl.BlockSpec(a.shape, lambda i: (0,) * a.ndim)
    row, col = count.reshape(1, toks), count.reshape(toks, 1)
    gain = gain.reshape(1, width)
    return pl.pallas_call(
        functools.partial(token_kernel, head_dim=head_dim),
        grid=(peers,),
        in_specs=[whole(mid), whole(row), whole(col), whole(pool), whole(gain),
                  pl.BlockSpec((1,) + w.shape[1:], lambda i: (i, 0, 0))]
        + [pl.BlockSpec(memory_space=pl.ANY)] * len(after),
        out_specs=[
            pl.BlockSpec((local, samples, 3, head_dim, toks), lambda i: (i, 0, 0, 0, 0)),
            pl.BlockSpec((local, samples, head_dim, toks), lambda i: (i, 0, 0, 0)),
            pl.BlockSpec((samples, toks, width), lambda i: (0, 0, 0)),
        ],
        out_shape=[
            jax.ShapeDtypeStruct((heads, samples, 3, head_dim, toks), BF),
            jax.ShapeDtypeStruct((heads, samples, head_dim, toks), BF),
            jax.ShapeDtypeStruct((samples, toks, width), F32),
        ],
        scratch_shapes=[pltpu.VMEM((samples * toks, width), BF)],
        compiler_params=params(),
        cost_estimate=pl.CostEstimate(flops=6_000_000_000, bytes_accessed=8_000_000, transcendentals=1000),
        name="pool_and_project",
    )(mid, row, col, pool, gain, w, *after)


def attend_kernel(place_ref, qkv_ref, gathered_ref, *refs):
    pieces, (out_ref, keys_ref, values_ref) = refs[:-3], refs[-3:]
    peers, samples, _, head_dim, toks = qkv_ref.shape
    qblocks = out_ref.shape[0]
    width = gathered_ref.shape[2]
    per = width // toks
    step = pl.program_id(0)
    first = pl.num_programs(0) // 2
    chip, core = place_ref[0], place_ref[1]
    chips = len(pieces) // 2

    def load(order):
        for s in range(samples):
            for i, p in enumerate(order):
                lanes = slice(i * toks, (i + 1) * toks)
                keys_ref[s, :, lanes] = qkv_ref[p, s, 1]
                values_ref[s, :head_dim, lanes] = qkv_ref[p, s, 2]
            values_ref[s, head_dim:, :] = jnp.ones((values_ref.shape[1] - head_dim, peers * toks), BF)

    def attend(tiles):
        bias = jnp.concatenate(tiles, axis=1).astype(F32)
        for s in range(samples):
            queries = jnp.concatenate(
                [qkv_ref[step * qblocks + j, s, 0] for j in range(qblocks)], axis=1
            )
            scores = dot(queries, keys_ref[s], (0, 0)) + bias
            top = jnp.max(scores, axis=1, keepdims=True)
            weights = jnp.exp2(scores - top).astype(BF)
            mixed = dot(weights, values_ref[s], (1, 1))
            mixed = mixed / mixed[:, head_dim : head_dim + 1]
            turned = mixed.T
            for j in range(qblocks):
                out_ref[j, s] = turned[:head_dim, j * toks : (j + 1) * toks].astype(BF)

    @pl.when(step == 0)
    def _():
        load(list(range(peers)))

    @pl.when(step == first)
    def _():
        order = []
        for i in range(2 * chips):
            source = lax.rem(chip + chips - i % chips, chips) * 2 + (core if i < chips else 1 - core)
            order += [source * per + j for j in range(per)]
        load(order)

    @pl.when(step < first)
    def _():
        attend([gathered_ref[c] for c in range(gathered_ref.shape[0])])

    @pl.when(step >= first)
    def _():
        attend([piece[...] for piece in pieces])


def token_attention(place, qkv, gathered, pieces):
    peers, samples, _, head_dim, toks = qkv.shape
    cols, rows, width = gathered.shape
    qblocks = 2
    tile = qblocks * toks
    keys = peers * toks
    first = rows // tile
    late = lambda i: (jnp.maximum(i - first, 0), 0)
    return pl.pallas_call(
        attend_kernel,
        grid=(2 * first,),
        in_specs=[
            pl.BlockSpec(memory_space=pltpu.SMEM),
            pl.BlockSpec(qkv.shape, lambda i: (0, 0, 0, 0, 0)),
            pl.BlockSpec((cols, tile, width), lambda i: (0, jnp.minimum(i, first - 1), 0)),
        ] + [pl.BlockSpec((tile, width), late)] * len(pieces),
        out_specs=pl.BlockSpec((qblocks, samples, head_dim, toks), lambda i: (i, 0, 0, 0)),
        out_shape=jax.ShapeDtypeStruct((peers, samples, head_dim, toks), BF),
        scratch_shapes=[
            pltpu.VMEM((samples, head_dim, keys), BF),
            pltpu.VMEM((samples, head_dim + 16, keys), BF),
        ],
        compiler_params=params(58 * 1024 * 1024),
        cost_estimate=pl.CostEstimate(
            flops=4 * samples * keys * keys * 128, bytes_accessed=2 * keys * keys + 2 * qkv.size,
            transcendentals=samples * keys * keys,
        ),
        name="token_attention",
    )(place, qkv, gathered, *pieces)


def out_kernel(mixed_ref, gate_ref, single_ref, out_proj_ref, return_ref, back_ref):
    heads, samples, head_dim, toks = mixed_ref.shape
    for s in range(samples):
        gate = jax.nn.sigmoid(gate_ref[:, s].astype(F32))
        gated = (gate * mixed_ref[:, s].astype(F32)).astype(BF).reshape(heads * head_dim, toks)
        new = single_ref[s] + dot(gated, out_proj_ref[...], (0, 0))
        back_ref[s] = jnp.dot(new.astype(BF), return_ref[...], preferred_element_type=F32).astype(BF)


def out_project(mixed, gate, single, out_proj, return_proj):
    return pl.pallas_call(
        out_kernel,
        out_shape=jax.ShapeDtypeStruct(single.shape[:2] + return_proj.shape[1:], BF),
        compiler_params=pltpu.CompilerParams(vmem_limit_bytes=VMEM_LIMIT),
        cost_estimate=pl.CostEstimate(flops=400_000_000, bytes_accessed=4_000_000, transcendentals=200_000),
        name="out_project",
    )(mixed, gate, single, out_proj, return_proj)


def spread_kernel(tok_ref, back_ref, mid_ref, out_ref):
    samples, atoms, channels = mid_ref.shape
    toks = back_ref.shape[1]
    col = lax.broadcasted_iota(jnp.int32, (atoms, toks), 1)
    onehot = jnp.where(col == tok_ref[...], 1.0, 0.0).astype(BF)
    for s in range(samples):
        spread = jnp.dot(onehot, back_ref[s], preferred_element_type=F32)
        out_ref[s] = (mid_ref[s].astype(F32) + spread).astype(BF)


def spread_back(local_tok, back, mid):
    return pl.pallas_call(
        spread_kernel,
        out_shape=jax.ShapeDtypeStruct(mid.shape, BF),
        compiler_params=pltpu.CompilerParams(vmem_limit_bytes=VMEM_LIMIT),
        cost_estimate=pl.CostEstimate(flops=100_000_000, bytes_accessed=2_000_000, transcendentals=0),
        name="spread_back",
    )(local_tok, back, mid)


def shards(
    atom_feats, atom_pair, key_shift, atom_token, token_count, atom_gain, atom_qkv,
    atom_out_proj, atom_pair_proj, pool_proj, token_gain, token_qkvg, pair_tiles, pair_proj,
    token_out_proj, return_proj,
):
    samples, atoms, channels = atom_feats.shape
    toks = token_count.shape[0]
    width = token_qkvg.shape[0]
    heads = pair_proj.shape[1]
    peers = lax.axis_size("col")
    seqs = lax.axis_size("seq")
    devices = peers * seqs
    qblock, window = atom_pair.shape[2:]
    margin = window // 2 - qblock // 2 + qblock

    up = [(i, i + 1) for i in range(devices - 1)]
    down = [(j, i) for i, j in up]
    before = lax.ppermute(atom_feats, ("seq", "col"), up)
    after = lax.ppermute(atom_feats, ("seq", "col"), down)

    turned_w = jnp.transpose(token_qkvg, (1, 2, 0)).reshape(-1, width)
    all_w = lax.all_gather(turned_w, "col", axis=0)

    tile_bias = jnp.einsum("ijc,ch->hij", pair_tiles, pair_proj, preferred_element_type=F32)
    tile_bias = (tile_bias * LOG2E).astype(BF)
    head_bias = lax.all_to_all(tile_bias, "seq", split_axis=0, concat_axis=0, tiled=True)

    index = lax.axis_index(("seq", "col"))
    offset = (index * atoms).astype(jnp.int32).reshape(1)
    mid = atom_attention(
        atom_feats, before, after, atom_pair, key_shift, offset, atoms * devices,
        atom_gain.reshape(1, -1), atom_qkv, atom_out_proj, atom_pair_proj.astype(F32),
    )
    head_bias = tie(head_bias.reshape(seqs * toks, -1), mid)
    half = seqs * toks // 2
    gathered = lax.all_gather(head_bias[:half], "col", axis=0)
    rest = head_bias[half:]
    chips = peers // 2
    pieces = [rest]
    for hop in range(1, chips):
        pairs = [(2 * x + k, 2 * ((x + hop) % chips) + k) for x in range(chips) for k in range(2)]
        pieces.append(lax.ppermute(rest, "col", pairs))

    mine = lax.all_to_all(
        mid.reshape(peers, samples // peers, atoms, channels), "col", split_axis=0, concat_axis=0, tiled=True
    )
    qkv, gate, single = pool_and_project(mine, token_count, pool_proj, token_gain, all_w, heads, (pieces[1], pieces[3]))
    swap = [(i, i ^ 1) for i in range(peers)]
    pieces += [lax.ppermute(tie(piece, single), "col", swap) for piece in pieces]
    qkv = lax.all_to_all(qkv, "seq", split_axis=0, concat_axis=0, tiled=True)
    col = lax.axis_index("col")
    place = jnp.stack([col // 2, col % 2]).astype(jnp.int32)
    mixed = token_attention(place, qkv, gathered, pieces)
    mixed = lax.all_to_all(mixed, "seq", split_axis=0, concat_axis=0, tiled=True)
    back = out_project(mixed, gate, single, token_out_proj, return_proj)
    back = lax.all_gather(back, "col", axis=0, tiled=True)
    local_tok = (atom_token - lax.axis_index("seq") * toks).reshape(atoms, 1)
    return spread_back(local_tok, back, mid)


def solution(mesh):
    placed = (
        P(None, ("seq", "col"), None),
        P(None, ("seq", "col"), None, None),
        P(("seq", "col")),
        P(("seq", "col")),
        P("seq"),
        P(),
        P(),
        P(),
        P(),
        P(),
        P(),
        P(None, None, "col"),
        P("seq", "col", None),
        P(),
        P(),
        P(),
    )
    return jax.shard_map(
        shards, mesh=mesh, in_specs=placed, out_specs=P(None, ("seq", "col"), None), check_vma=False
    )
```

```python
import functools

import jax
import jax.numpy as jnp
import numpy as np
from jax import lax
from jax.experimental import pallas as pl
from jax.experimental.pallas import tpu as pltpu
from jax.sharding import PartitionSpec as P

EPSILON = 1e-05
LOG2E = float(np.log2(np.e))
VMEM_LIMIT = 48 * 1024 * 1024
BF = jnp.bfloat16
F32 = jnp.float32


def params(limit=VMEM_LIMIT):
    return pltpu.CompilerParams(dimension_semantics=("arbitrary",), vmem_limit_bytes=limit)


def layer_norm(values, norm_gain):
    centred = values - jnp.mean(values, axis=-1, keepdims=True)
    variance = jnp.mean(centred * centred, axis=-1, keepdims=True)
    return centred * lax.rsqrt(variance + EPSILON) * norm_gain


def dot(a, b, contract):
    return lax.dot_general(a, b, ((contract[0:1], contract[1:2]), ((), ())), preferred_element_type=F32)


def atom_kernel(
    shift_ref, off_ref, wpair_ref, feats_ref, before_ref, after_ref, pair_ref, gain_ref,
    qkv_ref, out_proj_ref, mid_ref, bias_ref, kv_ref, *, limit_atoms,
):
    samples, atoms, channels = feats_ref.shape
    cpair, blocks, qblock, window = pair_ref.shape
    margin = window // 2 - qblock // 2 + qblock
    heads = wpair_ref.shape[1]
    head_dim = channels // heads
    rows = atoms + 2 * margin

    @pl.when(pl.program_id(0) == 0)
    def _():
        lane = lax.broadcasted_iota(jnp.int32, (qblock, window), 1)
        for b in range(blocks):
            tiles = [pair_ref[c, b].astype(F32) for c in range(cpair)]
            key = off_ref[0] - margin + qblock * (b + 1 + shift_ref[b]) + lane
            ok = (key >= 0) & (key < limit_atoms)
            for h in range(heads):
                acc = tiles[0] * wpair_ref[0, h]
                for c in range(1, cpair):
                    acc = acc + tiles[c] * wpair_ref[c, h]
                bias_ref[b, h * qblock : (h + 1) * qblock, :] = jnp.where(ok, acc * LOG2E, -1e9)

    feats = feats_ref[...]
    stacked = jnp.concatenate(
        [before_ref[:, atoms - margin :], feats, after_ref[:, :margin]], axis=1
    )
    flat = stacked.reshape(samples * rows, channels).astype(F32)
    normed = layer_norm(flat, gain_ref[...]).astype(BF)
    projected = jnp.dot(normed, qkv_ref[...], preferred_element_type=F32)
    kv_ref[...] = projected[:, channels:].astype(BF).reshape(samples, rows, 2 * channels)
    scale = LOG2E / float(np.sqrt(head_dim))
    queries = (projected[:, :channels] * scale).astype(BF).reshape(samples, rows, channels)
    lane_head = lax.broadcasted_iota(jnp.int32, (qblock, channels), 1) // head_dim
    masks = [lane_head == h for h in range(heads)]
    ones = jnp.ones((window, channels), BF)
    zero = jnp.zeros((qblock, channels), BF)
    attended = []
    pairs = [(s, b) for s in range(samples) for b in range(blocks)]
    group = 8
    for first in range(0, len(pairs), group):
        part = pairs[first : first + group]
        wins = [
            kv_ref[s, pl.ds(pl.multiple_of(qblock * (b + 1 + shift_ref[b]), qblock), window), :]
            for s, b in part
        ]
        scores = []
        for (s, b), win in zip(part, wins):
            q = queries[s, margin + b * qblock : margin + (b + 1) * qblock, :]
            spread = jnp.concatenate([jnp.where(m, q, zero) for m in masks], axis=0)
            scores.append(dot(spread, win[:, :channels], (1, 1)) + bias_ref[b])
        weights = [jnp.exp2(x - jnp.max(x, axis=1, keepdims=True)).astype(BF) for x in scores]
        for win, x in zip(wins, weights):
            both = jnp.concatenate([win[:, channels:], ones], axis=1)
            mixed = jnp.dot(x, both, preferred_element_type=F32)
            out = mixed[:qblock]
            for h in range(1, heads):
                own = mixed[h * qblock : (h + 1) * qblock]
                out = jnp.where(jnp.concatenate([masks[h], masks[h]], axis=1), own, out)
            attended.append((out[:, :channels] / out[:, channels:]).astype(BF))
    attended = jnp.concatenate(attended, axis=0)
    update = jnp.dot(attended, out_proj_ref[...], preferred_element_type=F32)
    mid = feats.reshape(samples * atoms, channels).astype(F32) + update
    mid_ref[...] = mid.astype(BF).reshape(samples, atoms, channels)


def atom_attention(feats, before, after, pair, shift, offset, limit, gain, qkv, out_proj, wpair):
    samples, atoms, channels = feats.shape
    blocks, qblock, window = pair.shape[1:]
    rows = atoms + 2 * (window // 2 - qblock // 2 + qblock)
    step = 8
    whole = lambda a: pl.BlockSpec(a.shape, lambda i: (0,) * a.ndim)
    part = lambda a: pl.BlockSpec((step,) + a.shape[1:], lambda i: (i, 0, 0))
    smem = pl.BlockSpec(memory_space=pltpu.SMEM)
    return pl.pallas_call(
        functools.partial(atom_kernel, limit_atoms=limit),
        grid=(samples // step,),
        in_specs=[smem, smem, smem, part(feats), part(before), part(after), whole(pair),
                  whole(gain), whole(qkv), whole(out_proj)],
        out_specs=part(feats),
        out_shape=jax.ShapeDtypeStruct(feats.shape, BF),
        scratch_shapes=[
            pltpu.VMEM((blocks, qblock * wpair.shape[1], window), F32),
            pltpu.VMEM((step, rows, 2 * channels), BF),
        ],
        compiler_params=params(),
        cost_estimate=pl.CostEstimate(flops=8_000_000_000, bytes_accessed=3_000_000, transcendentals=1_000_000),
        name="atom_attention",
    )(shift, offset, wpair, feats, before, after, pair, gain, qkv, out_proj)


def tie(value, *others):
    def kernel(*refs):
        pass
    hbm = pl.BlockSpec(memory_space=pl.ANY)
    return pl.pallas_call(
        kernel,
        in_specs=[hbm] * (1 + len(others)),
        out_specs=hbm,
        out_shape=jax.ShapeDtypeStruct(value.shape, value.dtype),
        input_output_aliases={0: 0},
        name="tie",
    )(value, *others)


def tie(value, *others):
    def kernel(*refs):
        pass
    hbm = pl.BlockSpec(memory_space=pl.ANY)
    return pl.pallas_call(
        kernel,
        in_specs=[hbm] * (1 + len(others)),
        out_specs=hbm,
        out_shape=jax.ShapeDtypeStruct(value.shape, value.dtype),
        input_output_aliases={0: 0},
        name="tie",
    )(value, *others)


def split_kernel(value_ref, after_ref, first_ref, rest_ref, sems):
    rows = first_ref.shape[0]
    copies = [
        pltpu.make_async_copy(value_ref.at[pl.ds(0, rows)], first_ref, sems.at[0]),
        pltpu.make_async_copy(value_ref.at[pl.ds(rows, rest_ref.shape[0])], rest_ref, sems.at[1]),
    ]
    for copy in copies:
        copy.start()
    for copy in copies:
        copy.wait()


def split_rows(value, rows, after):
    hbm = pl.BlockSpec(memory_space=pl.ANY)
    total, width = value.shape
    return pl.pallas_call(
        split_kernel,
        in_specs=[pl.BlockSpec(memory_space=pltpu.VMEM), hbm],
        out_specs=[hbm] * 2,
        out_shape=[
            jax.ShapeDtypeStruct((rows, width), value.dtype),
            jax.ShapeDtypeStruct((total - rows, width), value.dtype),
        ],
        scratch_shapes=[pltpu.SemaphoreType.DMA((2,))],
        cost_estimate=pl.CostEstimate(flops=0, bytes_accessed=4 * value.size, transcendentals=0),
        name="split_rows",
    )(value, after)


def token_kernel(
    mid_ref, count_row_ref, count_col_ref, pool_ref, gain_ref, w_hbm, qkv_ref, gate_ref,
    single_ref, normed_ref, w_ref, sem, *, head_dim,
):
    load = pltpu.make_async_copy(w_hbm, w_ref, sem)
    load.start()
    peers, samples, atoms, channels = mid_ref.shape
    toks = count_col_ref.shape[0]
    total = peers * atoms
    counts = count_col_ref[...]
    row = lax.broadcasted_iota(jnp.int32, (toks, toks), 0)
    col = lax.broadcasted_iota(jnp.int32, (toks, toks), 1)
    spread = jnp.broadcast_to(count_row_ref[...], (toks, toks))
    ends = jnp.sum(jnp.where(col <= row, spread, 0.0), axis=1, keepdims=True)
    begins = ends - counts
    atom = lax.broadcasted_iota(jnp.int32, (toks, total), 1).astype(F32)
    onehot = jnp.where((atom >= begins) & (atom < ends), 1.0, 0.0).astype(BF)
    for s in range(samples):
        mid = mid_ref[:, s].reshape(total, channels)
        lifted = jnp.dot(mid, pool_ref[...], preferred_element_type=F32)
        lifted = jnp.maximum(lifted, 0.0).astype(BF)
        single = jnp.dot(onehot, lifted, preferred_element_type=F32) / counts
        single_ref[s] = single
        normed_ref[s * toks : (s + 1) * toks, :] = layer_norm(single, gain_ref[...]).astype(BF)

    load.wait()
    scale = LOG2E / float(np.sqrt(head_dim))
    width = w_ref.shape[1] // 4
    local = width // head_dim
    for p in range(peers):
        turned = dot(w_ref[p], normed_ref[...], (1, 1))
        for hh in range(local):
            for s in range(samples):
                for f in range(4):
                    lo = f * width + hh * head_dim
                    tile = turned[lo : lo + head_dim, s * toks : (s + 1) * toks]
                    if f == 0:
                        tile = tile * scale
                    if f < 3:
                        qkv_ref[p * local + hh, s, f] = tile.astype(BF)
                    else:
                        gate_ref[p * local + hh, s] = tile.astype(BF)


def pool_and_project(mid, count, pool, gain, w, heads):
    peers, samples, atoms, channels = mid.shape
    toks = count.shape[0]
    width = pool.shape[1]
    head_dim = width // heads
    count = count.astype(F32)
    row, col = count.reshape(1, toks), count.reshape(toks, 1)
    gain = gain.reshape(1, width)
    vmem = pl.BlockSpec(memory_space=pltpu.VMEM)
    return pl.pallas_call(
        functools.partial(token_kernel, head_dim=head_dim),
        in_specs=[vmem] * 5 + [pl.BlockSpec(memory_space=pl.ANY)],
        out_specs=[vmem] * 3,
        out_shape=[
            jax.ShapeDtypeStruct((heads, samples, 3, head_dim, toks), BF),
            jax.ShapeDtypeStruct((heads, samples, head_dim, toks), BF),
            jax.ShapeDtypeStruct((samples, toks, width), F32),
        ],
        scratch_shapes=[
            pltpu.VMEM((samples * toks, width), BF),
            pltpu.VMEM(w.shape, BF),
            pltpu.SemaphoreType.DMA,
        ],
        compiler_params=pltpu.CompilerParams(vmem_limit_bytes=VMEM_LIMIT),
        cost_estimate=pl.CostEstimate(flops=6_000_000_000, bytes_accessed=8_000_000, transcendentals=1000),
        name="pool_and_project",
    )(mid, row, col, pool, gain, w)


def attend_kernel(place_ref, qkv_ref, gathered_ref, *refs, gathered_rows):
    pieces, (out_ref, keys_ref, values_ref) = refs[:-3], refs[-3:]
    peers, samples, _, head_dim, toks = qkv_ref.shape
    qblocks = out_ref.shape[0]
    width = gathered_ref.shape[2]
    per = width // toks
    step = pl.program_id(0)
    first = gathered_rows // (qblocks * toks)
    chip, core = place_ref[0], place_ref[1]
    chips = len(pieces) // 2

    def load(order):
        for s in range(samples):
            for i, p in enumerate(order):
                lanes = slice(i * toks, (i + 1) * toks)
                keys_ref[s, :, lanes] = qkv_ref[p, s, 1]
                values_ref[s, :head_dim, lanes] = qkv_ref[p, s, 2]
            values_ref[s, head_dim:, :] = jnp.ones((values_ref.shape[1] - head_dim, peers * toks), BF)

    def attend(tiles):
        for s in range(samples):
            queries = jnp.concatenate(
                [qkv_ref[step * qblocks + j, s, 0] for j in range(qblocks)], axis=1
            ).T
            top = None
            for i, tile in enumerate(tiles):
                lanes = slice(i * width, (i + 1) * width)
                scores = dot(queries, keys_ref[s, :, lanes], (1, 0)) + tile[...].astype(F32)
                peak = jnp.max(scores, axis=1, keepdims=True)
                if i > 0:
                    peak = jnp.maximum(top, peak)
                weights = jnp.exp2(scores - peak).astype(BF)
                part = dot(weights, values_ref[s, :, lanes], (1, 1))
                mixed = part if i == 0 else mixed * jnp.exp2(top - peak) + part
                top = peak
            turned = (mixed / mixed[:, head_dim : head_dim + 1]).T
            for j in range(qblocks):
                out_ref[j, s] = turned[:head_dim, j * toks : (j + 1) * toks].astype(BF)

    @pl.when(step == 0)
    def _():
        load(list(range(peers)))

    @pl.when(step == first)
    def _():
        order = []
        for i in range(2 * chips):
            source = lax.rem(chip + chips - i % chips, chips) * 2 + (core if i < chips else 1 - core)
            order += [source * per + j for j in range(per)]
        load(order)

    @pl.when(step < first)
    def _():
        attend([gathered_ref.at[c] for c in range(gathered_ref.shape[0])])

    @pl.when(step >= first)
    def _():
        attend(pieces)


def token_attention(place, qkv, gathered, pieces):
    peers, samples, _, head_dim, toks = qkv.shape
    cols, rows, width = gathered.shape
    qblocks = 4
    tile = qblocks * toks
    keys = peers * toks
    first = rows // tile
    late = lambda i: (jnp.maximum(i - first, 0), 0)
    return pl.pallas_call(
        functools.partial(attend_kernel, gathered_rows=rows),
        grid=(keys // tile,),
        in_specs=[
            pl.BlockSpec(memory_space=pltpu.SMEM),
            pl.BlockSpec(qkv.shape, lambda i: (0, 0, 0, 0, 0)),
            pl.BlockSpec((cols, tile, width), lambda i: (0, jnp.minimum(i, first - 1), 0)),
        ] + [pl.BlockSpec((tile, width), late)] * len(pieces),
        out_specs=pl.BlockSpec((qblocks, samples, head_dim, toks), lambda i: (i, 0, 0, 0)),
        out_shape=jax.ShapeDtypeStruct((peers, samples, head_dim, toks), BF),
        scratch_shapes=[
            pltpu.VMEM((samples, head_dim, keys), BF),
            pltpu.VMEM((samples, head_dim + 16, keys), BF),
        ],
        compiler_params=params(58 * 1024 * 1024),
        cost_estimate=pl.CostEstimate(
            flops=4 * samples * keys * keys * 128, bytes_accessed=2 * keys * keys + 2 * qkv.size,
            transcendentals=samples * keys * keys,
        ),
        name="token_attention",
    )(place, qkv, gathered, *pieces)


def out_kernel(mixed_ref, gate_ref, single_ref, out_proj_ref, return_ref, back_ref):
    heads, samples, head_dim, toks = mixed_ref.shape
    for s in range(samples):
        gate = jax.nn.sigmoid(gate_ref[:, s].astype(F32))
        gated = (gate * mixed_ref[:, s].astype(F32)).astype(BF).reshape(heads * head_dim, toks)
        new = single_ref[s] + dot(gated, out_proj_ref[...], (0, 0))
        back_ref[s] = jnp.dot(new.astype(BF), return_ref[...], preferred_element_type=F32).astype(BF)


def out_project(mixed, gate, single, out_proj, return_proj):
    return pl.pallas_call(
        out_kernel,
        out_shape=jax.ShapeDtypeStruct(single.shape[:2] + return_proj.shape[1:], BF),
        compiler_params=pltpu.CompilerParams(vmem_limit_bytes=VMEM_LIMIT),
        cost_estimate=pl.CostEstimate(flops=400_000_000, bytes_accessed=4_000_000, transcendentals=200_000),
        name="out_project",
    )(mixed, gate, single, out_proj, return_proj)


def spread_kernel(tok_ref, back_ref, mid_ref, out_ref):
    samples, atoms, channels = mid_ref.shape
    toks = back_ref.shape[1]
    col = lax.broadcasted_iota(jnp.int32, (atoms, toks), 1)
    onehot = jnp.where(col == tok_ref[...], 1.0, 0.0).astype(BF)
    for s in range(samples):
        spread = jnp.dot(onehot, back_ref[s], preferred_element_type=F32)
        out_ref[s] = (mid_ref[s].astype(F32) + spread).astype(BF)


def spread_back(local_tok, back, mid):
    return pl.pallas_call(
        spread_kernel,
        out_shape=jax.ShapeDtypeStruct(mid.shape, BF),
        compiler_params=pltpu.CompilerParams(vmem_limit_bytes=VMEM_LIMIT),
        cost_estimate=pl.CostEstimate(flops=100_000_000, bytes_accessed=2_000_000, transcendentals=0),
        name="spread_back",
    )(local_tok, back, mid)


def shards(
    atom_feats, atom_pair, key_shift, atom_token, token_count, atom_gain, atom_qkv,
    atom_out_proj, atom_pair_proj, pool_proj, token_gain, token_qkvg, pair_tiles, pair_proj,
    token_out_proj, return_proj,
):
    samples, atoms, channels = atom_feats.shape
    toks = token_count.shape[0]
    width = token_qkvg.shape[0]
    heads = pair_proj.shape[1]
    peers = lax.axis_size("col")
    seqs = lax.axis_size("seq")
    devices = peers * seqs
    qblock, window = atom_pair.shape[2:]
    margin = window // 2 - qblock // 2 + qblock

    up = [(i, i + 1) for i in range(devices - 1)]
    down = [(j, i) for i, j in up]
    before = lax.ppermute(atom_feats, ("seq", "col"), up)
    after = lax.ppermute(atom_feats, ("seq", "col"), down)

    turned_w = jnp.transpose(token_qkvg, (1, 2, 0)).reshape(-1, width)
    all_w = lax.all_gather(turned_w, "col", axis=0)

    tile_bias = jnp.einsum("ijc,ch->hij", pair_tiles, pair_proj, preferred_element_type=F32)
    tile_bias = (tile_bias * LOG2E).astype(BF)
    head_bias = lax.all_to_all(tile_bias, "seq", split_axis=0, concat_axis=0, tiled=True)

    index = lax.axis_index(("seq", "col"))
    offset = (index * atoms).astype(jnp.int32).reshape(1)
    mid = atom_attention(
        atom_feats, before, after, atom_pair, key_shift, offset, atoms * devices,
        atom_gain.reshape(1, -1), atom_qkv, atom_out_proj, atom_pair_proj.astype(F32),
    )
    chips = peers // 2
    first, rest = split_rows(head_bias.reshape(seqs * toks, -1), 3 * seqs * toks // 4, mid)
    gathered = lax.all_gather(first, "col", axis=0)

    mine = lax.all_to_all(
        mid.reshape(peers, samples // peers, atoms, channels), "col", split_axis=0, concat_axis=0, tiled=True
    )
    qkv, gate, single = pool_and_project(mine, token_count, pool_proj, token_gain, all_w, heads)
    pieces = [tie(rest, single)]
    for hop in range(1, chips):
        pairs = [(2 * x + k, 2 * ((x + hop) % chips) + k) for x in range(chips) for k in range(2)]
        pieces.append(lax.ppermute(pieces[0], "col", pairs))
    swap = [(i, i ^ 1) for i in range(peers)]
    pieces += [lax.ppermute(piece, "col", swap) for piece in pieces]
    qkv = lax.all_to_all(qkv, "seq", split_axis=0, concat_axis=0, tiled=True)
    col = lax.axis_index("col")
    place = jnp.stack([col // 2, col % 2]).astype(jnp.int32)
    mixed = token_attention(place, qkv, gathered, pieces)
    mixed = lax.all_to_all(mixed, "seq", split_axis=0, concat_axis=0, tiled=True)
    back = out_project(mixed, gate, single, token_out_proj, return_proj)
    back = lax.all_gather(back, "col", axis=0, tiled=True)
    local_tok = (atom_token - lax.axis_index("seq") * toks).reshape(atoms, 1)
    return spread_back(local_tok, back, mid)


def solution(mesh):
    placed = (
        P(None, ("seq", "col"), None),
        P(None, ("seq", "col"), None, None),
        P(("seq", "col")),
        P(("seq", "col")),
        P("seq"),
        P(),
        P(),
        P(),
        P(),
        P(),
        P(),
        P(None, None, "col"),
        P("seq", "col", None),
        P(),
        P(),
        P(),
    )
    return jax.shard_map(
        shards, mesh=mesh, in_specs=placed, out_specs=P(None, ("seq", "col"), None), check_vma=False
    )
```

```python
import functools

import jax
import jax.numpy as jnp
import numpy as np
from jax import lax
from jax.experimental import pallas as pl
from jax.experimental.pallas import tpu as pltpu
from jax.sharding import PartitionSpec as P

EPSILON = 1e-05
LOG2E = float(np.log2(np.e))
VMEM_LIMIT = 48 * 1024 * 1024
VMEM_MOST = 60 * 1024 * 1024
BF = jnp.bfloat16
F32 = jnp.float32


def params(limit=VMEM_LIMIT):
    return pltpu.CompilerParams(dimension_semantics=("arbitrary",), vmem_limit_bytes=limit)


def layer_norm(values, norm_gain):
    centred = values - jnp.mean(values, axis=-1, keepdims=True)
    variance = jnp.mean(centred * centred, axis=-1, keepdims=True)
    return centred * lax.rsqrt(variance + EPSILON) * norm_gain


def dot(a, b, contract):
    return lax.dot_general(a, b, ((contract[0:1], contract[1:2]), ((), ())), preferred_element_type=F32)


def atom_kernel(
    shift_ref, off_ref, wpair_ref, feats_ref, before_ref, after_ref, pair_ref, gain_ref,
    qkv_ref, out_proj_ref, *refs, limit_atoms,
):
    mid_ref, done_ref, bias_ref, kv_ref = refs[-4:]
    done_ref[...] = jnp.zeros_like(done_ref)
    samples, atoms, channels = feats_ref.shape
    cpair, blocks, qblock, window = pair_ref.shape
    margin = window // 2 - qblock // 2 + qblock
    heads = wpair_ref.shape[1]
    head_dim = channels // heads
    rows = atoms + 2 * margin

    @pl.when(pl.program_id(0) == 0)
    def _():
        lane = lax.broadcasted_iota(jnp.int32, (qblock, window), 1)
        for b in range(blocks):
            tiles = [pair_ref[c, b].astype(F32) for c in range(cpair)]
            key = off_ref[0] - margin + qblock * (b + 1 + shift_ref[b]) + lane
            ok = (key >= 0) & (key < limit_atoms)
            for h in range(heads):
                acc = tiles[0] * wpair_ref[0, h]
                for c in range(1, cpair):
                    acc = acc + tiles[c] * wpair_ref[c, h]
                bias_ref[b, h * qblock : (h + 1) * qblock, :] = jnp.where(ok, acc * LOG2E, -1e9)

    feats = feats_ref[...]
    stacked = jnp.concatenate(
        [before_ref[:, atoms - margin :], feats, after_ref[:, :margin]], axis=1
    )
    flat = stacked.reshape(samples * rows, channels).astype(F32)
    normed = layer_norm(flat, gain_ref[...]).astype(BF)
    projected = jnp.dot(normed, qkv_ref[...], preferred_element_type=F32)
    kv_ref[...] = projected[:, channels:].astype(BF).reshape(samples, rows, 2 * channels)
    scale = LOG2E / float(np.sqrt(head_dim))
    queries = (projected[:, :channels] * scale).astype(BF).reshape(samples, rows, channels)
    lane_head = lax.broadcasted_iota(jnp.int32, (qblock, channels), 1) // head_dim
    masks = [lane_head == h for h in range(heads)]
    ones = jnp.ones((window, channels), BF)
    zero = jnp.zeros((qblock, channels), BF)
    attended = []
    pairs = [(s, b) for s in range(samples) for b in range(blocks)]
    group = 8
    for first in range(0, len(pairs), group):
        part = pairs[first : first + group]
        wins = [
            kv_ref[s, pl.ds(pl.multiple_of(qblock * (b + 1 + shift_ref[b]), qblock), window), :]
            for s, b in part
        ]
        scores = []
        for (s, b), win in zip(part, wins):
            q = queries[s, margin + b * qblock : margin + (b + 1) * qblock, :]
            spread = jnp.concatenate([jnp.where(m, q, zero) for m in masks], axis=0)
            scores.append(dot(spread, win[:, :channels], (1, 1)) + bias_ref[b])
        weights = [jnp.exp2(x - jnp.max(x, axis=1, keepdims=True)).astype(BF) for x in scores]
        for win, x in zip(wins, weights):
            both = jnp.concatenate([win[:, channels:], ones], axis=1)
            mixed = jnp.dot(x, both, preferred_element_type=F32)
            out = mixed[:qblock]
            for h in range(1, heads):
                own = mixed[h * qblock : (h + 1) * qblock]
                out = jnp.where(jnp.concatenate([masks[h], masks[h]], axis=1), own, out)
            attended.append((out[:, :channels] / out[:, channels:]).astype(BF))
    attended = jnp.concatenate(attended, axis=0)
    update = jnp.dot(attended, out_proj_ref[...], preferred_element_type=F32)
    mid = feats.reshape(samples * atoms, channels).astype(F32) + update
    mid_ref[...] = mid.astype(BF).reshape(samples, atoms, channels)


def atom_attention(
    feats, before, after, pair, shift, offset, limit, gain, qkv, out_proj, wpair, others=()
):
    samples, atoms, channels = feats.shape
    blocks, qblock, window = pair.shape[1:]
    rows = atoms + 2 * (window // 2 - qblock // 2 + qblock)
    step = 8
    whole = lambda a: pl.BlockSpec(a.shape, lambda i: (0,) * a.ndim)
    part = lambda a: pl.BlockSpec((step,) + a.shape[1:], lambda i: (i, 0, 0))
    smem = pl.BlockSpec(memory_space=pltpu.SMEM)
    return pl.pallas_call(
        functools.partial(atom_kernel, limit_atoms=limit),
        grid=(samples // step,),
        in_specs=[smem, smem, smem, part(feats), part(before), part(after), whole(pair),
                  whole(gain), whole(qkv), whole(out_proj)]
        + [pl.BlockSpec(memory_space=pl.ANY)] * len(others),
        out_specs=[part(feats), pl.BlockSpec((8, 128), lambda i: (0, 0))],
        out_shape=[jax.ShapeDtypeStruct(feats.shape, BF), jax.ShapeDtypeStruct((8, 128), F32)],
        scratch_shapes=[
            pltpu.VMEM((blocks, qblock * wpair.shape[1], window), F32),
            pltpu.VMEM((step, rows, 2 * channels), BF),
        ],
        compiler_params=params(),
        cost_estimate=pl.CostEstimate(flops=8_000_000_000, bytes_accessed=3_000_000, transcendentals=1_000_000),
        name="atom_attention",
    )(shift, offset, wpair, feats, before, after, pair, gain, qkv, out_proj, *others)


def tie(value, after):
    def kernel(value_ref, after_ref, out_ref):
        pass

    hbm = pl.BlockSpec(memory_space=pl.ANY)
    return pl.pallas_call(
        kernel,
        in_specs=[hbm] * 2,
        out_specs=hbm,
        out_shape=jax.ShapeDtypeStruct(value.shape, value.dtype),
        input_output_aliases={0: 0},
        name="tie",
    )(value, after)


def split_kernel(value_ref, after_ref, first_ref, rest_ref):
    rows = first_ref.shape[0]
    first_ref[...] = value_ref[:rows]
    rest_ref[...] = value_ref[rows:]


def split_rows(value, rows, after):
    vmem = pl.BlockSpec(memory_space=pltpu.VMEM)
    total, width = value.shape
    return pl.pallas_call(
        split_kernel,
        in_specs=[vmem, pl.BlockSpec(memory_space=pl.ANY)],
        out_specs=[vmem] * 2,
        out_shape=[
            jax.ShapeDtypeStruct((rows, width), value.dtype),
            jax.ShapeDtypeStruct((total - rows, width), value.dtype),
        ],
        cost_estimate=pl.CostEstimate(flops=0, bytes_accessed=4 * value.size, transcendentals=0),
        name="split_rows",
    )(value, after)


def source_of(place_ref, i, peers):
    chips = peers // 2
    core = place_ref[1] if i < chips else 1 - place_ref[1]
    return lax.rem(place_ref[0] + chips - i % chips, chips) * 2 + core


def token_kernel(
    place_ref, mid_ref, count_row_ref, count_col_ref, pool_ref, gain_ref, *refs, head_dim, parts,
):
    qkv_ref, gate_ref, single_ref, normed_ref, w_ref, sems = refs[-6:]
    loads = []
    for i, (slot, row, rows) in enumerate(parts):
        dst = w_ref.at[slot, pl.ds(row, rows)]
        loads.append(pltpu.make_async_copy(refs[i], dst, sems.at[i]))
    for load in loads:
        load.start()
    peers, samples, atoms, channels = mid_ref.shape
    toks = count_col_ref.shape[0]
    total = peers * atoms
    counts = count_col_ref[...]
    row = lax.broadcasted_iota(jnp.int32, (toks, toks), 0)
    col = lax.broadcasted_iota(jnp.int32, (toks, toks), 1)
    spread = jnp.broadcast_to(count_row_ref[...], (toks, toks))
    ends = jnp.sum(jnp.where(col <= row, spread, 0.0), axis=1, keepdims=True)
    begins = ends - counts
    atom = lax.broadcasted_iota(jnp.int32, (toks, total), 1).astype(F32)
    onehot = jnp.where((atom >= begins) & (atom < ends), 1.0, 0.0).astype(BF)
    for s in range(samples):
        mid = mid_ref[:, s].reshape(total, channels)
        lifted = jnp.dot(mid, pool_ref[...], preferred_element_type=F32)
        lifted = jnp.maximum(lifted, 0.0).astype(BF)
        single = jnp.dot(onehot, lifted, preferred_element_type=F32) / counts
        single_ref[s] = single
        normed_ref[s * toks : (s + 1) * toks, :] = layer_norm(single, gain_ref[...]).astype(BF)

    for load in loads:
        load.wait()
    scale = LOG2E / float(np.sqrt(head_dim))
    width = w_ref.shape[1] // 4
    local = width // head_dim
    for i in range(peers):
        p = source_of(place_ref, i, peers)
        turned = dot(w_ref[i], normed_ref[...], (1, 1))
        for hh in range(local):
            for s in range(samples):
                for f in range(4):
                    lo = f * width + hh * head_dim
                    tile = turned[lo : lo + head_dim, s * toks : (s + 1) * toks]
                    if f == 0:
                        tile = tile * scale
                    if f < 3:
                        qkv_ref[p * local + hh, s, f] = tile.astype(BF)
                    else:
                        gate_ref[p * local + hh, s] = tile.astype(BF)


def pool_and_project(place, mid, count, pool, gain, pieces, heads, others):
    peers, samples, atoms, channels = mid.shape
    toks = count.shape[0]
    width = pool.shape[1]
    head_dim = width // heads
    count = count.astype(F32)
    row, col = count.reshape(1, toks), count.reshape(toks, 1)
    gain = gain.reshape(1, width)
    vmem = pl.BlockSpec(memory_space=pltpu.VMEM)
    hbm = pl.BlockSpec(memory_space=pl.ANY)
    parts = tuple((slot, first, array.shape[0]) for slot, first, array in pieces)
    return pl.pallas_call(
        functools.partial(token_kernel, head_dim=head_dim, parts=parts),
        in_specs=[pl.BlockSpec(memory_space=pltpu.SMEM)] + [vmem] * 5 + [hbm] * (len(pieces) + len(others)),
        out_specs=[vmem] * 3,
        out_shape=[
            jax.ShapeDtypeStruct((heads, samples, 3, head_dim, toks), BF),
            jax.ShapeDtypeStruct((heads, samples, head_dim, toks), BF),
            jax.ShapeDtypeStruct((samples, toks, width), F32),
        ],
        scratch_shapes=[
            pltpu.VMEM((samples * toks, width), BF),
            pltpu.VMEM((peers,) + pieces[0][2].shape, BF),
            pltpu.SemaphoreType.DMA((len(pieces),)),
        ],
        compiler_params=pltpu.CompilerParams(vmem_limit_bytes=VMEM_MOST),
        cost_estimate=pl.CostEstimate(flops=6_000_000_000, bytes_accessed=8_000_000, transcendentals=1000),
        name="pool_and_project",
    )(place, mid, row, col, pool, gain, *[array for _, _, array in pieces], *others)


def attend_kernel(place_ref, qkv_ref, *refs):
    out_ref, keys_ref, values_ref = refs[-3:]
    half = (len(refs) - 3) // 2
    upper, lower = refs[:half], refs[half : 2 * half]
    peers, samples, _, head_dim, toks = qkv_ref.shape
    qblocks = out_ref.shape[0]
    width = upper[0].shape[1]
    per = width // toks
    step = pl.program_id(0)
    first = pl.num_programs(0) // 2

    def load(order):
        for s in range(samples):
            for i, p in enumerate(order):
                lanes = slice(i * toks, (i + 1) * toks)
                keys_ref[s, :, lanes] = qkv_ref[p, s, 1]
                values_ref[s, :head_dim, lanes] = qkv_ref[p, s, 2]
            values_ref[s, head_dim:, :] = jnp.ones((values_ref.shape[1] - head_dim, peers * toks), BF)

    def attend(tiles):
        for s in range(samples):
            queries = jnp.concatenate(
                [qkv_ref[step * qblocks + j, s, 0] for j in range(qblocks)], axis=1
            ).T
            top = None
            for i, tile in enumerate(tiles):
                lanes = slice(i * width, (i + 1) * width)
                scores = dot(queries, keys_ref[s, :, lanes], (1, 0)) + tile[...].astype(F32)
                peak = jnp.max(scores, axis=1, keepdims=True)
                if i > 0:
                    peak = jnp.maximum(top, peak)
                weights = jnp.exp2(scores - peak).astype(BF)
                part = dot(weights, values_ref[s, :, lanes], (1, 1))
                mixed = part if i == 0 else mixed * jnp.exp2(top - peak) + part
                top = peak
            turned = (mixed / mixed[:, head_dim : head_dim + 1]).T
            for j in range(qblocks):
                out_ref[j, s] = turned[:head_dim, j * toks : (j + 1) * toks].astype(BF)

    @pl.when(step == 0)
    def _():
        sources = [source_of(place_ref, i, half) for i in range(half)]
        load([source * per + j for source in sources for j in range(per)])

    @pl.when(step < first)
    def _():
        attend(upper)

    @pl.when(step >= first)
    def _():
        attend(lower)


def token_attention(place, qkv, upper, lower):
    peers, samples, _, head_dim, toks = qkv.shape
    rows, width = upper[0].shape
    qblocks = 4
    tile = qblocks * toks
    keys = peers * toks
    first = rows // tile
    early = lambda i: (jnp.minimum(i, first - 1), 0)
    late = lambda i: (jnp.maximum(i - first, 0), 0)
    return pl.pallas_call(
        attend_kernel,
        grid=(keys // tile,),
        in_specs=[
            pl.BlockSpec(memory_space=pltpu.SMEM),
            pl.BlockSpec(qkv.shape, lambda i: (0, 0, 0, 0, 0)),
        ] + [pl.BlockSpec((tile, width), early)] * len(upper)
        + [pl.BlockSpec((tile, width), late)] * len(lower),
        out_specs=pl.BlockSpec((qblocks, samples, head_dim, toks), lambda i: (i, 0, 0, 0)),
        out_shape=jax.ShapeDtypeStruct((peers, samples, head_dim, toks), BF),
        scratch_shapes=[
            pltpu.VMEM((samples, head_dim, keys), BF),
            pltpu.VMEM((samples, head_dim + 16, keys), BF),
        ],
        compiler_params=params(VMEM_MOST),
        cost_estimate=pl.CostEstimate(
            flops=4 * samples * keys * keys * 128, bytes_accessed=2 * keys * keys + 2 * qkv.size,
            transcendentals=samples * keys * keys,
        ),
        name="token_attention",
    )(place, qkv, *upper, *lower)


def out_kernel(mixed_ref, gate_ref, single_ref, out_proj_ref, return_ref, back_ref):
    heads, samples, head_dim, toks = mixed_ref.shape
    for s in range(samples):
        gate = jax.nn.sigmoid(gate_ref[:, s].astype(F32))
        gated = (gate * mixed_ref[:, s].astype(F32)).astype(BF).reshape(heads * head_dim, toks)
        new = single_ref[s] + dot(gated, out_proj_ref[...], (0, 0))
        back_ref[s] = jnp.dot(new.astype(BF), return_ref[...], preferred_element_type=F32).astype(BF)


def out_project(mixed, gate, single, out_proj, return_proj):
    return pl.pallas_call(
        out_kernel,
        out_shape=jax.ShapeDtypeStruct(single.shape[:2] + return_proj.shape[1:], BF),
        compiler_params=pltpu.CompilerParams(vmem_limit_bytes=VMEM_LIMIT),
        cost_estimate=pl.CostEstimate(flops=400_000_000, bytes_accessed=4_000_000, transcendentals=200_000),
        name="out_project",
    )(mixed, gate, single, out_proj, return_proj)


def spread_kernel(tok_ref, back_ref, mid_ref, out_ref):
    samples, atoms, channels = mid_ref.shape
    toks = back_ref.shape[1]
    col = lax.broadcasted_iota(jnp.int32, (atoms, toks), 1)
    onehot = jnp.where(col == tok_ref[...], 1.0, 0.0).astype(BF)
    for s in range(samples):
        spread = jnp.dot(onehot, back_ref[s], preferred_element_type=F32)
        out_ref[s] = (mid_ref[s].astype(F32) + spread).astype(BF)


def spread_back(local_tok, back, mid):
    return pl.pallas_call(
        spread_kernel,
        out_shape=jax.ShapeDtypeStruct(mid.shape, BF),
        compiler_params=pltpu.CompilerParams(vmem_limit_bytes=VMEM_LIMIT),
        cost_estimate=pl.CostEstimate(flops=100_000_000, bytes_accessed=2_000_000, transcendentals=0),
        name="spread_back",
    )(local_tok, back, mid)


def shards(
    atom_feats, atom_pair, key_shift, atom_token, token_count, atom_gain, atom_qkv,
    atom_out_proj, atom_pair_proj, pool_proj, token_gain, token_qkvg, pair_tiles, pair_proj,
    token_out_proj, return_proj,
):
    samples, atoms, channels = atom_feats.shape
    toks = token_count.shape[0]
    width = token_qkvg.shape[0]
    heads = pair_proj.shape[1]
    peers = lax.axis_size("col")
    seqs = lax.axis_size("seq")
    devices = peers * seqs
    qblock, window = atom_pair.shape[2:]
    margin = window // 2 - qblock // 2 + qblock

    up = [(i, i + 1) for i in range(devices - 1)]
    down = [(j, i) for i, j in up]
    before = lax.ppermute(atom_feats, ("seq", "col"), up)
    after = lax.ppermute(atom_feats, ("seq", "col"), down)

    chips = peers // 2
    col = lax.axis_index("col")
    place = jnp.stack([col // 2, col % 2]).astype(jnp.int32)

    def along(value, hop):
        pairs = [(2 * x + k, 2 * ((x + hop) % chips) + k) for x in range(chips) for k in range(2)]
        return lax.ppermute(value, "col", pairs)

    def across(value):
        return lax.ppermute(value, "col", [(i, i ^ 1) for i in range(peers)])

    own_w = jnp.transpose(token_qkvg, (1, 2, 0)).reshape(-1, width)
    back_w, ahead_w = along(own_w, 1), along(own_w, -1)

    tile_bias = jnp.einsum("ijc,ch->hij", pair_tiles, pair_proj, preferred_element_type=F32)
    tile_bias = (tile_bias * LOG2E).astype(BF)
    head_bias = lax.all_to_all(tile_bias, "seq", split_axis=0, concat_axis=0, tiled=True)

    index = lax.axis_index(("seq", "col"))
    offset = (index * atoms).astype(jnp.int32).reshape(1)
    mid, done = atom_attention(
        atom_feats, before, after, atom_pair, key_shift, offset, atoms * devices,
        atom_gain.reshape(1, -1), atom_qkv, atom_out_proj, atom_pair_proj.astype(F32),
        (back_w, ahead_w),
    )
    mine = lax.all_to_all(
        mid.reshape(peers, samples // peers, atoms, channels), "col", split_axis=0, concat_axis=0, tiled=True
    )
    half = seqs * toks // 2
    upper, lower = split_rows(head_bias.reshape(seqs * toks, -1), half, done)
    pieces = [(0, 0, own_w), (1, 0, back_w), (2, 0, tie(along(own_w, 2), upper)), (3, 0, ahead_w)]
    pieces += [(slot + chips, first, across(array)) for slot, first, array in pieces]
    back_upper, ahead_lower = along(upper, 1), along(lower, -1)
    qkv, gate, single = pool_and_project(
        place, mine, token_count, pool_proj, token_gain, pieces, heads, (back_upper, ahead_lower)
    )
    back_lower, ahead_upper = along(lower, 1), along(upper, -1)
    uppers = [upper, back_upper, along(back_upper, 1), ahead_upper]
    lowers = [lower, back_lower, along(ahead_lower, -1), ahead_lower]
    qkv = lax.all_to_all(qkv, "seq", split_axis=0, concat_axis=0, tiled=True)
    uppers += [across(piece) for piece in uppers]
    lowers += [across(piece) for piece in lowers]
    mixed = token_attention(place, qkv, uppers, lowers)
    mixed = lax.all_to_all(mixed, "seq", split_axis=0, concat_axis=0, tiled=True)
    back = out_project(mixed, gate, single, token_out_proj, return_proj)
    back = lax.all_gather(back, "col", axis=0, tiled=True)
    local_tok = (atom_token - lax.axis_index("seq") * toks).reshape(atoms, 1)
    return spread_back(local_tok, back, mid)


def solution(mesh):
    placed = (
        P(None, ("seq", "col"), None),
        P(None, ("seq", "col"), None, None),
        P(("seq", "col")),
        P(("seq", "col")),
        P("seq"),
        P(),
        P(),
        P(),
        P(),
        P(),
        P(),
        P(None, None, "col"),
        P("seq", "col", None),
        P(),
        P(),
        P(),
    )
    return jax.shard_map(
        shards, mesh=mesh, in_specs=placed, out_specs=P(None, ("seq", "col"), None), check_vma=False
    )
```

```python
import functools

import jax
import jax.numpy as jnp
import numpy as np
from jax import lax
from jax.experimental import pallas as pl
from jax.experimental.pallas import tpu as pltpu
from jax.sharding import PartitionSpec as P

EPSILON = 1e-05
LOG2E = float(np.log2(np.e))
VMEM_LIMIT = 48 * 1024 * 1024
VMEM_MOST = 60 * 1024 * 1024
BF = jnp.bfloat16
F32 = jnp.float32


def params(limit=VMEM_LIMIT):
    return pltpu.CompilerParams(dimension_semantics=("arbitrary",), vmem_limit_bytes=limit)


def layer_norm(values, norm_gain):
    centred = values - jnp.mean(values, axis=-1, keepdims=True)
    variance = jnp.mean(centred * centred, axis=-1, keepdims=True)
    return centred * lax.rsqrt(variance + EPSILON) * norm_gain


def dot(a, b, contract):
    return lax.dot_general(a, b, ((contract[0:1], contract[1:2]), ((), ())), preferred_element_type=F32)


def atom_kernel(
    shift_ref, off_ref, wpair_ref, feats_ref, before_ref, after_ref, pair_ref, gain_ref,
    qkv_ref, out_proj_ref, *refs, limit_atoms,
):
    mid_ref, done_ref, bias_ref, kv_ref = refs[-4:]
    done_ref[...] = jnp.zeros_like(done_ref)
    samples, atoms, channels = feats_ref.shape
    cpair, blocks, qblock, window = pair_ref.shape
    margin = window // 2 - qblock // 2 + qblock
    heads = wpair_ref.shape[1]
    head_dim = channels // heads
    rows = atoms + 2 * margin

    @pl.when(pl.program_id(0) == 0)
    def _():
        lane = lax.broadcasted_iota(jnp.int32, (qblock, window), 1)
        for b in range(blocks):
            tiles = [pair_ref[c, b].astype(F32) for c in range(cpair)]
            key = off_ref[0] - margin + qblock * (b + 1 + shift_ref[b]) + lane
            ok = (key >= 0) & (key < limit_atoms)
            for h in range(heads):
                acc = tiles[0] * wpair_ref[0, h]
                for c in range(1, cpair):
                    acc = acc + tiles[c] * wpair_ref[c, h]
                bias_ref[b, h * qblock : (h + 1) * qblock, :] = jnp.where(ok, acc * LOG2E, -1e9)

    feats = feats_ref[...]
    stacked = jnp.concatenate(
        [before_ref[:, atoms - margin :], feats, after_ref[:, :margin]], axis=1
    )
    flat = stacked.reshape(samples * rows, channels).astype(F32)
    normed = layer_norm(flat, gain_ref[...]).astype(BF)
    projected = jnp.dot(normed, qkv_ref[...], preferred_element_type=F32)
    kv_ref[...] = projected[:, channels:].astype(BF).reshape(samples, rows, 2 * channels)
    scale = LOG2E / float(np.sqrt(head_dim))
    queries = (projected[:, :channels] * scale).astype(BF).reshape(samples, rows, channels)
    lane_head = lax.broadcasted_iota(jnp.int32, (qblock, channels), 1) // head_dim
    masks = [lane_head == h for h in range(heads)]
    ones = jnp.ones((window, channels), BF)
    zero = jnp.zeros((qblock, channels), BF)
    attended = []
    pairs = [(s, b) for s in range(samples) for b in range(blocks)]
    group = 8
    for first in range(0, len(pairs), group):
        part = pairs[first : first + group]
        wins = [
            kv_ref[s, pl.ds(pl.multiple_of(qblock * (b + 1 + shift_ref[b]), qblock), window), :]
            for s, b in part
        ]
        scores = []
        for (s, b), win in zip(part, wins):
            q = queries[s, margin + b * qblock : margin + (b + 1) * qblock, :]
            spread = jnp.concatenate([jnp.where(m, q, zero) for m in masks], axis=0)
            scores.append(dot(spread, win[:, :channels], (1, 1)) + bias_ref[b])
        weights = [jnp.exp2(x - jnp.max(x, axis=1, keepdims=True)).astype(BF) for x in scores]
        for win, x in zip(wins, weights):
            both = jnp.concatenate([win[:, channels:], ones], axis=1)
            mixed = jnp.dot(x, both, preferred_element_type=F32)
            out = mixed[:qblock]
            for h in range(1, heads):
                own = mixed[h * qblock : (h + 1) * qblock]
                out = jnp.where(jnp.concatenate([masks[h], masks[h]], axis=1), own, out)
            attended.append((out[:, :channels] / out[:, channels:]).astype(BF))
    attended = jnp.concatenate(attended, axis=0)
    update = jnp.dot(attended, out_proj_ref[...], preferred_element_type=F32)
    mid = feats.reshape(samples * atoms, channels).astype(F32) + update
    mid_ref[...] = mid.astype(BF).reshape(samples, atoms, channels)


def atom_attention(
    feats, before, after, pair, shift, offset, limit, gain, qkv, out_proj, wpair, others=()
):
    samples, atoms, channels = feats.shape
    blocks, qblock, window = pair.shape[1:]
    rows = atoms + 2 * (window // 2 - qblock // 2 + qblock)
    step = 8
    whole = lambda a: pl.BlockSpec(a.shape, lambda i: (0,) * a.ndim)
    part = lambda a: pl.BlockSpec((step,) + a.shape[1:], lambda i: (i, 0, 0))
    smem = pl.BlockSpec(memory_space=pltpu.SMEM)
    return pl.pallas_call(
        functools.partial(atom_kernel, limit_atoms=limit),
        grid=(samples // step,),
        in_specs=[smem, smem, smem, part(feats), part(before), part(after), whole(pair),
                  whole(gain), whole(qkv), whole(out_proj)]
        + [pl.BlockSpec(memory_space=pl.ANY)] * len(others),
        out_specs=[part(feats), pl.BlockSpec((8, 128), lambda i: (0, 0))],
        out_shape=[jax.ShapeDtypeStruct(feats.shape, BF), jax.ShapeDtypeStruct((8, 128), F32)],
        scratch_shapes=[
            pltpu.VMEM((blocks, qblock * wpair.shape[1], window), F32),
            pltpu.VMEM((step, rows, 2 * channels), BF),
        ],
        compiler_params=params(),
        cost_estimate=pl.CostEstimate(flops=8_000_000_000, bytes_accessed=3_000_000, transcendentals=1_000_000),
        name="atom_attention",
    )(shift, offset, wpair, feats, before, after, pair, gain, qkv, out_proj, *others)


def tie(value, after):
    def kernel(value_ref, after_ref, out_ref):
        pass

    hbm = pl.BlockSpec(memory_space=pl.ANY)
    return pl.pallas_call(
        kernel,
        in_specs=[hbm] * 2,
        out_specs=hbm,
        out_shape=jax.ShapeDtypeStruct(value.shape, value.dtype),
        input_output_aliases={0: 0},
        name="tie",
    )(value, after)


def source_of(place_ref, i, peers):
    chips = peers // 2
    core = place_ref[1] if i < chips else 1 - place_ref[1]
    return lax.rem(place_ref[0] + chips - i % chips, chips) * 2 + core


def token_kernel(
    place_ref, mid_ref, count_row_ref, count_col_ref, pool_ref, gain_ref, *refs, head_dim, parts,
):
    qkv_ref, gate_ref, single_ref, normed_ref, w_ref, sems = refs[-6:]
    loads = []
    for i, (slot, row, rows) in enumerate(parts):
        dst = w_ref.at[slot, pl.ds(row, rows)]
        loads.append(pltpu.make_async_copy(refs[i], dst, sems.at[i]))
    for load in loads:
        load.start()
    peers, samples, atoms, channels = mid_ref.shape
    toks = count_col_ref.shape[0]
    total = peers * atoms
    counts = count_col_ref[...]
    row = lax.broadcasted_iota(jnp.int32, (toks, toks), 0)
    col = lax.broadcasted_iota(jnp.int32, (toks, toks), 1)
    spread = jnp.broadcast_to(count_row_ref[...], (toks, toks))
    ends = jnp.sum(jnp.where(col <= row, spread, 0.0), axis=1, keepdims=True)
    begins = ends - counts
    atom = lax.broadcasted_iota(jnp.int32, (toks, total), 1).astype(F32)
    onehot = jnp.where((atom >= begins) & (atom < ends), 1.0, 0.0).astype(BF)
    for s in range(samples):
        mid = mid_ref[:, s].reshape(total, channels)
        lifted = jnp.dot(mid, pool_ref[...], preferred_element_type=F32)
        lifted = jnp.maximum(lifted, 0.0).astype(BF)
        single = jnp.dot(onehot, lifted, preferred_element_type=F32) / counts
        single_ref[s] = single
        normed_ref[s * toks : (s + 1) * toks, :] = layer_norm(single, gain_ref[...]).astype(BF)

    for load in loads:
        load.wait()
    scale = LOG2E / float(np.sqrt(head_dim))
    width = w_ref.shape[1] // 4
    local = width // head_dim
    for i in range(peers):
        p = source_of(place_ref, i, peers)
        turned = dot(w_ref[i], normed_ref[...], (1, 1))
        for hh in range(local):
            for s in range(samples):
                for f in range(4):
                    lo = f * width + hh * head_dim
                    tile = turned[lo : lo + head_dim, s * toks : (s + 1) * toks]
                    if f == 0:
                        tile = tile * scale
                    if f < 3:
                        qkv_ref[p * local + hh, s, f] = tile.astype(BF)
                    else:
                        gate_ref[p * local + hh, s] = tile.astype(BF)


def pool_and_project(place, mid, count, pool, gain, pieces, heads, others):
    peers, samples, atoms, channels = mid.shape
    toks = count.shape[0]
    width = pool.shape[1]
    head_dim = width // heads
    count = count.astype(F32)
    row, col = count.reshape(1, toks), count.reshape(toks, 1)
    gain = gain.reshape(1, width)
    vmem = pl.BlockSpec(memory_space=pltpu.VMEM)
    hbm = pl.BlockSpec(memory_space=pl.ANY)
    parts = tuple((slot, first, array.shape[0]) for slot, first, array in pieces)
    return pl.pallas_call(
        functools.partial(token_kernel, head_dim=head_dim, parts=parts),
        in_specs=[pl.BlockSpec(memory_space=pltpu.SMEM)] + [vmem] * 5 + [hbm] * (len(pieces) + len(others)),
        out_specs=[vmem] * 3,
        out_shape=[
            jax.ShapeDtypeStruct((heads, samples, 3, head_dim, toks), BF),
            jax.ShapeDtypeStruct((heads, samples, head_dim, toks), BF),
            jax.ShapeDtypeStruct((samples, toks, width), F32),
        ],
        scratch_shapes=[
            pltpu.VMEM((samples * toks, width), BF),
            pltpu.VMEM((peers,) + pieces[0][2].shape, BF),
            pltpu.SemaphoreType.DMA((len(pieces),)),
        ],
        compiler_params=pltpu.CompilerParams(vmem_limit_bytes=VMEM_MOST),
        cost_estimate=pl.CostEstimate(flops=6_000_000_000, bytes_accessed=8_000_000, transcendentals=1000),
        name="pool_and_project",
    )(place, mid, row, col, pool, gain, *[array for _, _, array in pieces], *others)


def attend_kernel(place_ref, qkv_ref, *refs):
    out_ref, keys_ref, values_ref = refs[-3:]
    halves = refs[-7:-3]
    chips = (len(refs) - 7) // 2 + 1
    half = 2 * chips
    upper, lower = list(refs[:-7]), list(refs[:-7])
    for core in range(2):
        upper.insert(core * chips + 2, halves[2 * core])
        lower.insert(core * chips + 2, halves[2 * core + 1])
    peers, samples, _, head_dim, toks = qkv_ref.shape
    qblocks = out_ref.shape[0]
    width = refs[0].shape[1]
    per = width // toks
    step = pl.program_id(0)
    first = pl.num_programs(0) // 2

    def load(order):
        for s in range(samples):
            for i, p in enumerate(order):
                lanes = slice(i * toks, (i + 1) * toks)
                keys_ref[s, :, lanes] = qkv_ref[p, s, 1]
                values_ref[s, :head_dim, lanes] = qkv_ref[p, s, 2]
            values_ref[s, head_dim:, :] = jnp.ones((values_ref.shape[1] - head_dim, peers * toks), BF)

    def attend(tiles):
        for s in range(samples):
            queries = jnp.concatenate(
                [qkv_ref[step * qblocks + j, s, 0] for j in range(qblocks)], axis=1
            ).T
            top = None
            for i, tile in enumerate(tiles):
                lanes = slice(i * width, (i + 1) * width)
                scores = dot(queries, keys_ref[s, :, lanes], (1, 0)) + tile[...].astype(F32)
                peak = jnp.max(scores, axis=1, keepdims=True)
                if i > 0:
                    peak = jnp.maximum(top, peak)
                weights = jnp.exp2(scores - peak).astype(BF)
                part = dot(weights, values_ref[s, :, lanes], (1, 1))
                mixed = part if i == 0 else mixed * jnp.exp2(top - peak) + part
                top = peak
            turned = (mixed / mixed[:, head_dim : head_dim + 1]).T
            for j in range(qblocks):
                out_ref[j, s] = turned[:head_dim, j * toks : (j + 1) * toks].astype(BF)

    @pl.when(step == 0)
    def _():
        sources = [source_of(place_ref, i, half) for i in range(half)]
        load([source * per + j for source in sources for j in range(per)])

    @pl.when(step < first)
    def _():
        attend(upper)

    @pl.when(step >= first)
    def _():
        attend(lower)


def token_attention(place, qkv, whole, halves):
    peers, samples, _, head_dim, toks = qkv.shape
    rows, width = halves[0].shape
    qblocks = 4
    tile = qblocks * toks
    keys = peers * toks
    first = rows // tile
    early = lambda i: (jnp.minimum(i, first - 1), 0)
    late = lambda i: (jnp.maximum(i - first, 0), 0)
    return pl.pallas_call(
        attend_kernel,
        grid=(keys // tile,),
        in_specs=[
            pl.BlockSpec(memory_space=pltpu.SMEM),
            pl.BlockSpec(qkv.shape, lambda i: (0, 0, 0, 0, 0)),
        ] + [pl.BlockSpec((tile, width), lambda i: (i, 0))] * len(whole)
        + [pl.BlockSpec((tile, width), early), pl.BlockSpec((tile, width), late)] * 2,
        out_specs=pl.BlockSpec((qblocks, samples, head_dim, toks), lambda i: (i, 0, 0, 0)),
        out_shape=jax.ShapeDtypeStruct((peers, samples, head_dim, toks), BF),
        scratch_shapes=[
            pltpu.VMEM((samples, head_dim, keys), BF),
            pltpu.VMEM((samples, head_dim + 16, keys), BF),
        ],
        compiler_params=params(VMEM_MOST),
        cost_estimate=pl.CostEstimate(
            flops=4 * samples * keys * keys * 128, bytes_accessed=2 * keys * keys + 2 * qkv.size,
            transcendentals=samples * keys * keys,
        ),
        name="token_attention",
    )(place, qkv, *whole, *halves)


def out_kernel(mixed_ref, gate_ref, single_ref, out_proj_ref, return_ref, back_ref):
    heads, samples, head_dim, toks = mixed_ref.shape
    for s in range(samples):
        gate = jax.nn.sigmoid(gate_ref[:, s].astype(F32))
        gated = (gate * mixed_ref[:, s].astype(F32)).astype(BF).reshape(heads * head_dim, toks)
        new = single_ref[s] + dot(gated, out_proj_ref[...], (0, 0))
        back_ref[s] = jnp.dot(new.astype(BF), return_ref[...], preferred_element_type=F32).astype(BF)


def out_project(mixed, gate, single, out_proj, return_proj):
    return pl.pallas_call(
        out_kernel,
        out_shape=jax.ShapeDtypeStruct(single.shape[:2] + return_proj.shape[1:], BF),
        compiler_params=pltpu.CompilerParams(vmem_limit_bytes=VMEM_LIMIT),
        cost_estimate=pl.CostEstimate(flops=400_000_000, bytes_accessed=4_000_000, transcendentals=200_000),
        name="out_project",
    )(mixed, gate, single, out_proj, return_proj)


def spread_kernel(tok_ref, back_ref, mid_ref, out_ref):
    samples, atoms, channels = mid_ref.shape
    toks = back_ref.shape[1]
    col = lax.broadcasted_iota(jnp.int32, (atoms, toks), 1)
    onehot = jnp.where(col == tok_ref[...], 1.0, 0.0).astype(BF)
    for s in range(samples):
        spread = jnp.dot(onehot, back_ref[s], preferred_element_type=F32)
        out_ref[s] = (mid_ref[s].astype(F32) + spread).astype(BF)


def spread_back(local_tok, back, mid):
    return pl.pallas_call(
        spread_kernel,
        out_shape=jax.ShapeDtypeStruct(mid.shape, BF),
        compiler_params=pltpu.CompilerParams(vmem_limit_bytes=VMEM_LIMIT),
        cost_estimate=pl.CostEstimate(flops=100_000_000, bytes_accessed=2_000_000, transcendentals=0),
        name="spread_back",
    )(local_tok, back, mid)


def shards(
    atom_feats, atom_pair, key_shift, atom_token, token_count, atom_gain, atom_qkv,
    atom_out_proj, atom_pair_proj, pool_proj, token_gain, token_qkvg, pair_tiles, pair_proj,
    token_out_proj, return_proj,
):
    samples, atoms, channels = atom_feats.shape
    toks = token_count.shape[0]
    width = token_qkvg.shape[0]
    heads = pair_proj.shape[1]
    peers = lax.axis_size("col")
    seqs = lax.axis_size("seq")
    devices = peers * seqs
    qblock, window = atom_pair.shape[2:]
    margin = window // 2 - qblock // 2 + qblock

    up = [(i, i + 1) for i in range(devices - 1)]
    down = [(j, i) for i, j in up]
    before = lax.ppermute(atom_feats, ("seq", "col"), up)
    after = lax.ppermute(atom_feats, ("seq", "col"), down)

    chips = peers // 2
    col = lax.axis_index("col")
    place = jnp.stack([col // 2, col % 2]).astype(jnp.int32)

    def along(value, hop):
        pairs = [(2 * x + k, 2 * ((x + hop) % chips) + k) for x in range(chips) for k in range(2)]
        return lax.ppermute(value, "col", pairs)

    def across(value):
        return lax.ppermute(value, "col", [(i, i ^ 1) for i in range(peers)])

    own_w = jnp.transpose(token_qkvg, (1, 2, 0)).reshape(-1, width)
    back_w, ahead_w = along(own_w, 1), along(own_w, -1)

    tile_bias = jnp.einsum("ijc,ch->hij", pair_tiles, pair_proj, preferred_element_type=F32)
    tile_bias = (tile_bias * LOG2E).astype(BF)
    head_bias = lax.all_to_all(tile_bias, "seq", split_axis=0, concat_axis=0, tiled=True)

    index = lax.axis_index(("seq", "col"))
    offset = (index * atoms).astype(jnp.int32).reshape(1)
    mid, done = atom_attention(
        atom_feats, before, after, atom_pair, key_shift, offset, atoms * devices,
        atom_gain.reshape(1, -1), atom_qkv, atom_out_proj, atom_pair_proj.astype(F32),
        (back_w, ahead_w),
    )
    mine = lax.all_to_all(
        mid.reshape(peers, samples // peers, atoms, channels), "col", split_axis=0, concat_axis=0, tiled=True
    )
    half = seqs * toks // 2
    own = tie(head_bias.reshape(seqs * toks, -1), done)
    back, ahead = along(own, 1), along(own, -1)
    passed = [along(back[:half], 1), along(ahead[half:], -1)]
    pieces = [(0, 0, own_w), (1, 0, back_w), (2, 0, tie(along(own_w, 2), own)), (3, 0, ahead_w)]
    pieces += [(slot + chips, first, across(array)) for slot, first, array in pieces]
    qkv, gate, single = pool_and_project(
        place, mine, token_count, pool_proj, token_gain, pieces, heads, (back, ahead)
    )
    whole = [own, back, ahead]
    qkv = lax.all_to_all(qkv, "seq", split_axis=0, concat_axis=0, tiled=True)
    whole += [across(piece) for piece in whole]
    halves = passed + [across(piece) for piece in passed]
    mixed = token_attention(place, qkv, whole, halves)
    mixed = lax.all_to_all(mixed, "seq", split_axis=0, concat_axis=0, tiled=True)
    back = out_project(mixed, gate, single, token_out_proj, return_proj)
    back = lax.all_gather(back, "col", axis=0, tiled=True)
    local_tok = (atom_token - lax.axis_index("seq") * toks).reshape(atoms, 1)
    return spread_back(local_tok, back, mid)


def solution(mesh):
    placed = (
        P(None, ("seq", "col"), None),
        P(None, ("seq", "col"), None, None),
        P(("seq", "col")),
        P(("seq", "col")),
        P("seq"),
        P(),
        P(),
        P(),
        P(),
        P(),
        P(),
        P(None, None, "col"),
        P("seq", "col", None),
        P(),
        P(),
        P(),
    )
    return jax.shard_map(
        shards, mesh=mesh, in_specs=placed, out_specs=P(None, ("seq", "col"), None), check_vma=False
    )
```

```python
import functools

import jax
import jax.numpy as jnp
import numpy as np
from jax import lax
from jax.experimental import pallas as pl
from jax.experimental.pallas import tpu as pltpu
from jax.sharding import PartitionSpec as P

EPSILON = 1e-05
LOG2E = float(np.log2(np.e))
VMEM_LIMIT = 48 * 1024 * 1024
VMEM_MOST = 60 * 1024 * 1024
BF = jnp.bfloat16
F32 = jnp.float32


def params(limit=VMEM_LIMIT):
    return pltpu.CompilerParams(dimension_semantics=("arbitrary",), vmem_limit_bytes=limit)


def layer_norm(values, norm_gain):
    centred = values - jnp.mean(values, axis=-1, keepdims=True)
    variance = jnp.mean(centred * centred, axis=-1, keepdims=True)
    return centred * lax.rsqrt(variance + EPSILON) * norm_gain


def dot(a, b, contract):
    return lax.dot_general(a, b, ((contract[0:1], contract[1:2]), ((), ())), preferred_element_type=F32)


def atom_kernel(
    shift_ref, off_ref, wpair_ref, feats_ref, before_ref, after_ref, pair_ref, gain_ref,
    qkv_ref, out_proj_ref, *refs, limit_atoms,
):
    mid_ref, done_ref, bias_ref, kv_ref = refs[-4:]
    done_ref[...] = jnp.zeros_like(done_ref)
    samples, atoms, channels = feats_ref.shape
    cpair, blocks, qblock, window = pair_ref.shape
    margin = window // 2 - qblock // 2 + qblock
    heads = wpair_ref.shape[1]
    head_dim = channels // heads
    rows = atoms + 2 * margin

    @pl.when(pl.program_id(0) == 0)
    def _():
        lane = lax.broadcasted_iota(jnp.int32, (qblock, window), 1)
        for b in range(blocks):
            tiles = [pair_ref[c, b].astype(F32) for c in range(cpair)]
            key = off_ref[0] - margin + qblock * (b + 1 + shift_ref[b]) + lane
            ok = (key >= 0) & (key < limit_atoms)
            for h in range(heads):
                acc = tiles[0] * wpair_ref[0, h]
                for c in range(1, cpair):
                    acc = acc + tiles[c] * wpair_ref[c, h]
                bias_ref[b, h * qblock : (h + 1) * qblock, :] = jnp.where(ok, acc * LOG2E, -1e9)

    feats = feats_ref[...]
    stacked = jnp.concatenate(
        [before_ref[:, atoms - margin :], feats, after_ref[:, :margin]], axis=1
    )
    flat = stacked.reshape(samples * rows, channels).astype(F32)
    normed = layer_norm(flat, gain_ref[...]).astype(BF)
    projected = jnp.dot(normed, qkv_ref[...], preferred_element_type=F32)
    kv_ref[...] = projected[:, channels:].astype(BF).reshape(samples, rows, 2 * channels)
    scale = LOG2E / float(np.sqrt(head_dim))
    queries = (projected[:, :channels] * scale).astype(BF).reshape(samples, rows, channels)
    lane_head = lax.broadcasted_iota(jnp.int32, (qblock, channels), 1) // head_dim
    masks = [lane_head == h for h in range(heads)]
    ones = jnp.ones((window, channels), BF)
    zero = jnp.zeros((qblock, channels), BF)
    attended = []
    pairs = [(s, b) for s in range(samples) for b in range(blocks)]
    group = 8
    for first in range(0, len(pairs), group):
        part = pairs[first : first + group]
        wins = [
            kv_ref[s, pl.ds(pl.multiple_of(qblock * (b + 1 + shift_ref[b]), qblock), window), :]
            for s, b in part
        ]
        scores = []
        for (s, b), win in zip(part, wins):
            q = queries[s, margin + b * qblock : margin + (b + 1) * qblock, :]
            spread = jnp.concatenate([jnp.where(m, q, zero) for m in masks], axis=0)
            scores.append(dot(spread, win[:, :channels], (1, 1)) + bias_ref[b])
        weights = [jnp.exp2(x - jnp.max(x, axis=1, keepdims=True)).astype(BF) for x in scores]
        for win, x in zip(wins, weights):
            both = jnp.concatenate([win[:, channels:], ones], axis=1)
            mixed = jnp.dot(x, both, preferred_element_type=F32)
            out = mixed[:qblock]
            for h in range(1, heads):
                own = mixed[h * qblock : (h + 1) * qblock]
                out = jnp.where(jnp.concatenate([masks[h], masks[h]], axis=1), own, out)
            attended.append((out[:, :channels] / out[:, channels:]).astype(BF))
    attended = jnp.concatenate(attended, axis=0)
    update = jnp.dot(attended, out_proj_ref[...], preferred_element_type=F32)
    mid = feats.reshape(samples * atoms, channels).astype(F32) + update
    mid_ref[...] = mid.astype(BF).reshape(samples, atoms, channels)


def atom_attention(
    feats, before, after, pair, shift, offset, limit, gain, qkv, out_proj, wpair, others=()
):
    samples, atoms, channels = feats.shape
    blocks, qblock, window = pair.shape[1:]
    rows = atoms + 2 * (window // 2 - qblock // 2 + qblock)
    step = 8
    whole = lambda a: pl.BlockSpec(a.shape, lambda i: (0,) * a.ndim)
    part = lambda a: pl.BlockSpec((step,) + a.shape[1:], lambda i: (i, 0, 0))
    smem = pl.BlockSpec(memory_space=pltpu.SMEM)
    return pl.pallas_call(
        functools.partial(atom_kernel, limit_atoms=limit),
        grid=(samples // step,),
        in_specs=[smem, smem, smem, part(feats), part(before), part(after), whole(pair),
                  whole(gain), whole(qkv), whole(out_proj)]
        + [pl.BlockSpec(memory_space=pl.ANY)] * len(others),
        out_specs=[part(feats), pl.BlockSpec((8, 128), lambda i: (0, 0))],
        out_shape=[jax.ShapeDtypeStruct(feats.shape, BF), jax.ShapeDtypeStruct((8, 128), F32)],
        scratch_shapes=[
            pltpu.VMEM((blocks, qblock * wpair.shape[1], window), F32),
            pltpu.VMEM((step, rows, 2 * channels), BF),
        ],
        compiler_params=params(),
        cost_estimate=pl.CostEstimate(flops=8_000_000_000, bytes_accessed=3_000_000, transcendentals=1_000_000),
        name="atom_attention",
    )(shift, offset, wpair, feats, before, after, pair, gain, qkv, out_proj, *others)


def tie(value, after):
    def kernel(value_ref, after_ref, out_ref):
        pass

    hbm = pl.BlockSpec(memory_space=pl.ANY)
    return pl.pallas_call(
        kernel,
        in_specs=[hbm] * 2,
        out_specs=hbm,
        out_shape=jax.ShapeDtypeStruct(value.shape, value.dtype),
        input_output_aliases={0: 0},
        name="tie",
    )(value, after)


def split_kernel(value_ref, after_ref, first_ref, rest_ref):
    rows = first_ref.shape[0]
    first_ref[...] = value_ref[:rows]
    rest_ref[...] = value_ref[rows:]


def split_rows(value, rows, after):
    vmem = pl.BlockSpec(memory_space=pltpu.VMEM)
    total, width = value.shape
    return pl.pallas_call(
        split_kernel,
        in_specs=[vmem, pl.BlockSpec(memory_space=pl.ANY)],
        out_specs=[vmem] * 2,
        out_shape=[
            jax.ShapeDtypeStruct((rows, width), value.dtype),
            jax.ShapeDtypeStruct((total - rows, width), value.dtype),
        ],
        cost_estimate=pl.CostEstimate(flops=0, bytes_accessed=4 * value.size, transcendentals=0),
        name="split_rows",
    )(value, after)


def source_of(place_ref, i, peers):
    chips = peers // 2
    core = place_ref[1] if i < chips else 1 - place_ref[1]
    return lax.rem(place_ref[0] + chips - i % chips, chips) * 2 + core


def token_kernel(
    place_ref, mid_ref, count_row_ref, count_col_ref, pool_ref, gain_ref, *refs, head_dim, parts,
):
    qkv_ref, gate_ref, single_ref, normed_ref, w_ref, sems = refs[-6:]
    loads = []
    for i, (slot, row, rows) in enumerate(parts):
        dst = w_ref.at[slot, pl.ds(row, rows)]
        loads.append(pltpu.make_async_copy(refs[i], dst, sems.at[i]))
    for load in loads:
        load.start()
    peers, samples, atoms, channels = mid_ref.shape
    toks = count_col_ref.shape[0]
    total = peers * atoms
    counts = count_col_ref[...]
    row = lax.broadcasted_iota(jnp.int32, (toks, toks), 0)
    col = lax.broadcasted_iota(jnp.int32, (toks, toks), 1)
    spread = jnp.broadcast_to(count_row_ref[...], (toks, toks))
    ends = jnp.sum(jnp.where(col <= row, spread, 0.0), axis=1, keepdims=True)
    begins = ends - counts
    atom = lax.broadcasted_iota(jnp.int32, (toks, total), 1).astype(F32)
    onehot = jnp.where((atom >= begins) & (atom < ends), 1.0, 0.0).astype(BF)
    for s in range(samples):
        mid = mid_ref[:, s].reshape(total, channels)
        lifted = jnp.dot(mid, pool_ref[...], preferred_element_type=F32)
        lifted = jnp.maximum(lifted, 0.0).astype(BF)
        single = jnp.dot(onehot, lifted, preferred_element_type=F32) / counts
        single_ref[s] = single
        normed_ref[s * toks : (s + 1) * toks, :] = layer_norm(single, gain_ref[...]).astype(BF)

    for load in loads:
        load.wait()
    scale = LOG2E / float(np.sqrt(head_dim))
    width = w_ref.shape[1] // 4
    local = width // head_dim
    for i in range(peers):
        p = source_of(place_ref, i, peers)
        turned = dot(w_ref[i], normed_ref[...], (1, 1))
        for hh in range(local):
            for s in range(samples):
                for f in range(4):
                    lo = f * width + hh * head_dim
                    tile = turned[lo : lo + head_dim, s * toks : (s + 1) * toks]
                    if f == 0:
                        tile = tile * scale
                    if f < 3:
                        qkv_ref[p * local + hh, s, f] = tile.astype(BF)
                    else:
                        gate_ref[p * local + hh, s] = tile.astype(BF)


def pool_and_project(place, mid, count, pool, gain, pieces, heads, others):
    peers, samples, atoms, channels = mid.shape
    toks = count.shape[0]
    width = pool.shape[1]
    head_dim = width // heads
    count = count.astype(F32)
    row, col = count.reshape(1, toks), count.reshape(toks, 1)
    gain = gain.reshape(1, width)
    vmem = pl.BlockSpec(memory_space=pltpu.VMEM)
    hbm = pl.BlockSpec(memory_space=pl.ANY)
    parts = tuple((slot, first, array.shape[0]) for slot, first, array in pieces)
    return pl.pallas_call(
        functools.partial(token_kernel, head_dim=head_dim, parts=parts),
        in_specs=[pl.BlockSpec(memory_space=pltpu.SMEM)] + [vmem] * 5 + [hbm] * (len(pieces) + len(others)),
        out_specs=[vmem] * 3,
        out_shape=[
            jax.ShapeDtypeStruct((heads, samples, 3, head_dim, toks), BF),
            jax.ShapeDtypeStruct((heads, samples, head_dim, toks), BF),
            jax.ShapeDtypeStruct((samples, toks, width), F32),
        ],
        scratch_shapes=[
            pltpu.VMEM((samples * toks, width), BF),
            pltpu.VMEM((peers,) + pieces[0][2].shape, BF),
            pltpu.SemaphoreType.DMA((len(pieces),)),
        ],
        compiler_params=pltpu.CompilerParams(vmem_limit_bytes=VMEM_MOST),
        cost_estimate=pl.CostEstimate(flops=6_000_000_000, bytes_accessed=8_000_000, transcendentals=1000),
        name="pool_and_project",
    )(place, mid, row, col, pool, gain, *[array for _, _, array in pieces], *others)


def attend_kernel(place_ref, qkv_ref, *refs):
    out_ref, keys_ref, values_ref = refs[-3:]
    half = (len(refs) - 3) // 2
    upper, lower = refs[:half], refs[half : 2 * half]
    peers, samples, _, head_dim, toks = qkv_ref.shape
    qblocks = out_ref.shape[0]
    width = upper[0].shape[1]
    per = width // toks
    step = pl.program_id(0)
    first = pl.num_programs(0) // 2

    def load(order):
        for s in range(samples):
            for i, p in enumerate(order):
                lanes = slice(i * toks, (i + 1) * toks)
                keys_ref[s, :, lanes] = qkv_ref[p, s, 1]
                values_ref[s, :head_dim, lanes] = qkv_ref[p, s, 2]
            values_ref[s, head_dim:, :] = jnp.ones((values_ref.shape[1] - head_dim, peers * toks), BF)

    def attend(tiles):
        for s in range(samples):
            queries = jnp.concatenate(
                [qkv_ref[step * qblocks + j, s, 0] for j in range(qblocks)], axis=1
            ).T
            top = None
            for i, tile in enumerate(tiles):
                lanes = slice(i * width, (i + 1) * width)
                scores = dot(queries, keys_ref[s, :, lanes], (1, 0)) + tile[...].astype(F32)
                peak = jnp.max(scores, axis=1, keepdims=True)
                if i > 0:
                    peak = jnp.maximum(top, peak)
                weights = jnp.exp2(scores - peak).astype(BF)
                part = dot(weights, values_ref[s, :, lanes], (1, 1))
                mixed = part if i == 0 else mixed * jnp.exp2(top - peak) + part
                top = peak
            turned = (mixed / mixed[:, head_dim : head_dim + 1]).T
            for j in range(qblocks):
                out_ref[j, s] = turned[:head_dim, j * toks : (j + 1) * toks].astype(BF)

    @pl.when(step == 0)
    def _():
        sources = [source_of(place_ref, i, half) for i in range(half)]
        load([source * per + j for source in sources for j in range(per)])

    @pl.when(step < first)
    def _():
        attend(upper)

    @pl.when(step >= first)
    def _():
        attend(lower)


def token_attention(place, qkv, upper, lower):
    peers, samples, _, head_dim, toks = qkv.shape
    rows, width = upper[0].shape
    qblocks = 4
    tile = qblocks * toks
    keys = peers * toks
    first = rows // tile
    early = lambda i: (jnp.minimum(i, first - 1), 0)
    late = lambda i: (jnp.maximum(i - first, 0), 0)
    return pl.pallas_call(
        attend_kernel,
        grid=(keys // tile,),
        in_specs=[
            pl.BlockSpec(memory_space=pltpu.SMEM),
            pl.BlockSpec(qkv.shape, lambda i: (0, 0, 0, 0, 0)),
        ] + [pl.BlockSpec((tile, width), early)] * len(upper)
        + [pl.BlockSpec((tile, width), late)] * len(lower),
        out_specs=pl.BlockSpec((qblocks, samples, head_dim, toks), lambda i: (i, 0, 0, 0)),
        out_shape=jax.ShapeDtypeStruct((peers, samples, head_dim, toks), BF),
        scratch_shapes=[
            pltpu.VMEM((samples, head_dim, keys), BF),
            pltpu.VMEM((samples, head_dim + 16, keys), BF),
        ],
        compiler_params=params(VMEM_MOST),
        cost_estimate=pl.CostEstimate(
            flops=4 * samples * keys * keys * 128, bytes_accessed=2 * keys * keys + 2 * qkv.size,
            transcendentals=samples * keys * keys,
        ),
        name="token_attention",
    )(place, qkv, *upper, *lower)


def out_kernel(mixed_ref, gate_ref, single_ref, out_proj_ref, return_ref, back_ref):
    heads, samples, head_dim, toks = mixed_ref.shape
    for s in range(samples):
        gate = jax.nn.sigmoid(gate_ref[:, s].astype(F32))
        gated = (gate * mixed_ref[:, s].astype(F32)).astype(BF).reshape(heads * head_dim, toks)
        new = single_ref[s] + dot(gated, out_proj_ref[...], (0, 0))
        back_ref[s] = jnp.dot(new.astype(BF), return_ref[...], preferred_element_type=F32).astype(BF)


def out_project(mixed, gate, single, out_proj, return_proj):
    return pl.pallas_call(
        out_kernel,
        out_shape=jax.ShapeDtypeStruct(single.shape[:2] + return_proj.shape[1:], BF),
        compiler_params=pltpu.CompilerParams(vmem_limit_bytes=VMEM_LIMIT),
        cost_estimate=pl.CostEstimate(flops=400_000_000, bytes_accessed=4_000_000, transcendentals=200_000),
        name="out_project",
    )(mixed, gate, single, out_proj, return_proj)


def spread_kernel(tok_ref, back_ref, mid_ref, out_ref):
    samples, atoms, channels = mid_ref.shape
    toks = back_ref.shape[1]
    col = lax.broadcasted_iota(jnp.int32, (atoms, toks), 1)
    onehot = jnp.where(col == tok_ref[...], 1.0, 0.0).astype(BF)
    for s in range(samples):
        spread = jnp.dot(onehot, back_ref[s], preferred_element_type=F32)
        out_ref[s] = (mid_ref[s].astype(F32) + spread).astype(BF)


def spread_back(local_tok, back, mid):
    return pl.pallas_call(
        spread_kernel,
        out_shape=jax.ShapeDtypeStruct(mid.shape, BF),
        compiler_params=pltpu.CompilerParams(vmem_limit_bytes=VMEM_LIMIT),
        cost_estimate=pl.CostEstimate(flops=100_000_000, bytes_accessed=2_000_000, transcendentals=0),
        name="spread_back",
    )(local_tok, back, mid)


def shards(
    atom_feats, atom_pair, key_shift, atom_token, token_count, atom_gain, atom_qkv,
    atom_out_proj, atom_pair_proj, pool_proj, token_gain, token_qkvg, pair_tiles, pair_proj,
    token_out_proj, return_proj,
):
    samples, atoms, channels = atom_feats.shape
    toks = token_count.shape[0]
    width = token_qkvg.shape[0]
    heads = pair_proj.shape[1]
    peers = lax.axis_size("col")
    seqs = lax.axis_size("seq")
    devices = peers * seqs
    qblock, window = atom_pair.shape[2:]
    margin = window // 2 - qblock // 2 + qblock

    up = [(i, i + 1) for i in range(devices - 1)]
    down = [(j, i) for i, j in up]
    before = lax.ppermute(atom_feats, ("seq", "col"), up)
    after = lax.ppermute(atom_feats, ("seq", "col"), down)

    chips = peers // 2
    col = lax.axis_index("col")
    place = jnp.stack([col // 2, col % 2]).astype(jnp.int32)

    def along(value, hop):
        pairs = [(2 * x + k, 2 * ((x + hop) % chips) + k) for x in range(chips) for k in range(2)]
        return lax.ppermute(value, "col", pairs)

    def across(value):
        return lax.ppermute(value, "col", [(i, i ^ 1) for i in range(peers)])

    own_w = jnp.transpose(token_qkvg, (1, 2, 0)).reshape(-1, width)
    back_w, ahead_w = along(own_w, 1), along(own_w, -1)

    tile_bias = jnp.einsum("ijc,ch->hij", pair_tiles, pair_proj, preferred_element_type=F32)
    tile_bias = (tile_bias * LOG2E).astype(BF)
    head_bias = lax.all_to_all(tile_bias, "seq", split_axis=0, concat_axis=0, tiled=True)

    index = lax.axis_index(("seq", "col"))
    offset = (index * atoms).astype(jnp.int32).reshape(1)
    mid, done = atom_attention(
        atom_feats, before, after, atom_pair, key_shift, offset, atoms * devices,
        atom_gain.reshape(1, -1), atom_qkv, atom_out_proj, atom_pair_proj.astype(F32),
        (back_w, ahead_w),
    )
    mine = lax.all_to_all(
        mid.reshape(peers, samples // peers, atoms, channels), "col", split_axis=0, concat_axis=0, tiled=True
    )
    half = seqs * toks // 2
    upper, lower = split_rows(head_bias.reshape(seqs * toks, -1), half, done)
    pieces = [(0, 0, own_w), (1, 0, back_w), (2, 0, tie(along(own_w, 2), upper)), (3, 0, ahead_w)]
    pieces += [(slot + chips, first, across(array)) for slot, first, array in pieces]
    back_upper, ahead_lower = along(upper, 1), along(lower, -1)
    qkv, gate, single = pool_and_project(
        place, mine, token_count, pool_proj, token_gain, pieces, heads, ()
    )
    back_lower, ahead_upper = along(lower, 1), along(upper, -1)
    uppers = [upper, back_upper, along(back_upper, 1), ahead_upper]
    lowers = [lower, back_lower, along(ahead_lower, -1), ahead_lower]
    qkv = lax.all_to_all(qkv, "seq", split_axis=0, concat_axis=0, tiled=True)
    uppers += [across(piece) for piece in uppers]
    lowers += [across(piece) for piece in lowers]
    mixed = token_attention(place, qkv, uppers, lowers)
    mixed = lax.all_to_all(mixed, "seq", split_axis=0, concat_axis=0, tiled=True)
    back = out_project(mixed, gate, single, token_out_proj, return_proj)
    back = lax.all_gather(back, "col", axis=0, tiled=True)
    local_tok = (atom_token - lax.axis_index("seq") * toks).reshape(atoms, 1)
    return spread_back(local_tok, back, mid)


def solution(mesh):
    placed = (
        P(None, ("seq", "col"), None),
        P(None, ("seq", "col"), None, None),
        P(("seq", "col")),
        P(("seq", "col")),
        P("seq"),
        P(),
        P(),
        P(),
        P(),
        P(),
        P(),
        P(None, None, "col"),
        P("seq", "col", None),
        P(),
        P(),
        P(),
    )
    return jax.shard_map(
        shards, mesh=mesh, in_specs=placed, out_specs=P(None, ("seq", "col"), None), check_vma=False
    )
```

```python
import functools

import jax
import jax.numpy as jnp
import numpy as np
from jax import lax
from jax.experimental import pallas as pl
from jax.experimental.pallas import tpu as pltpu
from jax.sharding import PartitionSpec as P

EPSILON = 1e-05
LOG2E = float(np.log2(np.e))
VMEM_LIMIT = 48 * 1024 * 1024
VMEM_MOST = 60 * 1024 * 1024
BF = jnp.bfloat16
F32 = jnp.float32


def params(limit=VMEM_LIMIT):
    return pltpu.CompilerParams(dimension_semantics=("arbitrary",), vmem_limit_bytes=limit)


def layer_norm(values, norm_gain):
    centred = values - jnp.mean(values, axis=-1, keepdims=True)
    variance = jnp.mean(centred * centred, axis=-1, keepdims=True)
    return centred * lax.rsqrt(variance + EPSILON) * norm_gain


def dot(a, b, contract):
    return lax.dot_general(a, b, ((contract[0:1], contract[1:2]), ((), ())), preferred_element_type=F32)


def atom_kernel(
    shift_ref, off_ref, wpair_ref, feats_ref, before_ref, after_ref, pair_ref, gain_ref,
    qkv_ref, out_proj_ref, *refs, limit_atoms,
):
    mid_ref, done_ref, bias_ref, kv_ref = refs[-4:]
    done_ref[...] = jnp.zeros_like(done_ref)
    samples, atoms, channels = feats_ref.shape
    cpair, blocks, qblock, window = pair_ref.shape
    margin = window // 2 - qblock // 2 + qblock
    heads = wpair_ref.shape[1]
    head_dim = channels // heads
    rows = atoms + 2 * margin

    @pl.when(pl.program_id(0) == 0)
    def _():
        lane = lax.broadcasted_iota(jnp.int32, (qblock, window), 1)
        for b in range(blocks):
            tiles = [pair_ref[c, b].astype(F32) for c in range(cpair)]
            key = off_ref[0] - margin + qblock * (b + 1 + shift_ref[b]) + lane
            ok = (key >= 0) & (key < limit_atoms)
            for h in range(heads):
                acc = tiles[0] * wpair_ref[0, h]
                for c in range(1, cpair):
                    acc = acc + tiles[c] * wpair_ref[c, h]
                bias_ref[b, h * qblock : (h + 1) * qblock, :] = jnp.where(ok, acc * LOG2E, -1e9)

    feats = feats_ref[...]
    stacked = jnp.concatenate(
        [before_ref[:, atoms - margin :], feats, after_ref[:, :margin]], axis=1
    )
    flat = stacked.reshape(samples * rows, channels).astype(F32)
    normed = layer_norm(flat, gain_ref[...]).astype(BF)
    projected = jnp.dot(normed, qkv_ref[...], preferred_element_type=F32)
    kv_ref[...] = projected[:, channels:].astype(BF).reshape(samples, rows, 2 * channels)
    scale = LOG2E / float(np.sqrt(head_dim))
    queries = (projected[:, :channels] * scale).astype(BF).reshape(samples, rows, channels)
    lane_head = lax.broadcasted_iota(jnp.int32, (qblock, channels), 1) // head_dim
    masks = [lane_head == h for h in range(heads)]
    ones = jnp.ones((window, channels), BF)
    zero = jnp.zeros((qblock, channels), BF)
    attended = []
    pairs = [(s, b) for s in range(samples) for b in range(blocks)]
    group = 8
    for first in range(0, len(pairs), group):
        part = pairs[first : first + group]
        wins = [
            kv_ref[s, pl.ds(pl.multiple_of(qblock * (b + 1 + shift_ref[b]), qblock), window), :]
            for s, b in part
        ]
        scores = []
        for (s, b), win in zip(part, wins):
            q = queries[s, margin + b * qblock : margin + (b + 1) * qblock, :]
            spread = jnp.concatenate([jnp.where(m, q, zero) for m in masks], axis=0)
            scores.append(dot(spread, win[:, :channels], (1, 1)) + bias_ref[b])
        weights = [jnp.exp2(x - jnp.max(x, axis=1, keepdims=True)).astype(BF) for x in scores]
        for win, x in zip(wins, weights):
            both = jnp.concatenate([win[:, channels:], ones], axis=1)
            mixed = jnp.dot(x, both, preferred_element_type=F32)
            out = mixed[:qblock]
            for h in range(1, heads):
                own = mixed[h * qblock : (h + 1) * qblock]
                out = jnp.where(jnp.concatenate([masks[h], masks[h]], axis=1), own, out)
            attended.append((out[:, :channels] / out[:, channels:]).astype(BF))
    attended = jnp.concatenate(attended, axis=0)
    update = jnp.dot(attended, out_proj_ref[...], preferred_element_type=F32)
    mid = feats.reshape(samples * atoms, channels).astype(F32) + update
    mid_ref[...] = mid.astype(BF).reshape(samples, atoms, channels)


def atom_attention(
    feats, before, after, pair, shift, offset, limit, gain, qkv, out_proj, wpair, others=()
):
    samples, atoms, channels = feats.shape
    blocks, qblock, window = pair.shape[1:]
    rows = atoms + 2 * (window // 2 - qblock // 2 + qblock)
    step = 8
    whole = lambda a: pl.BlockSpec(a.shape, lambda i: (0,) * a.ndim)
    part = lambda a: pl.BlockSpec((step,) + a.shape[1:], lambda i: (i, 0, 0))
    smem = pl.BlockSpec(memory_space=pltpu.SMEM)
    return pl.pallas_call(
        functools.partial(atom_kernel, limit_atoms=limit),
        grid=(samples // step,),
        in_specs=[smem, smem, smem, part(feats), part(before), part(after), whole(pair),
                  whole(gain), whole(qkv), whole(out_proj)]
        + [pl.BlockSpec(memory_space=pl.ANY)] * len(others),
        out_specs=[part(feats), pl.BlockSpec((8, 128), lambda i: (0, 0))],
        out_shape=[jax.ShapeDtypeStruct(feats.shape, BF), jax.ShapeDtypeStruct((8, 128), F32)],
        scratch_shapes=[
            pltpu.VMEM((blocks, qblock * wpair.shape[1], window), F32),
            pltpu.VMEM((step, rows, 2 * channels), BF),
        ],
        compiler_params=params(),
        cost_estimate=pl.CostEstimate(flops=8_000_000_000, bytes_accessed=3_000_000, transcendentals=1_000_000),
        name="atom_attention",
    )(shift, offset, wpair, feats, before, after, pair, gain, qkv, out_proj, *others)


def tie(value, after):
    def kernel(value_ref, after_ref, out_ref):
        pass

    hbm = pl.BlockSpec(memory_space=pl.ANY)
    return pl.pallas_call(
        kernel,
        in_specs=[hbm] * 2,
        out_specs=hbm,
        out_shape=jax.ShapeDtypeStruct(value.shape, value.dtype),
        input_output_aliases={0: 0},
        name="tie",
    )(value, after)


def split_kernel(value_ref, after_ref, first_ref, rest_ref):
    rows = first_ref.shape[0]
    first_ref[...] = value_ref[:rows]
    rest_ref[...] = value_ref[rows:]


def split_rows(value, rows, after):
    vmem = pl.BlockSpec(memory_space=pltpu.VMEM)
    total, width = value.shape
    return pl.pallas_call(
        split_kernel,
        in_specs=[vmem, pl.BlockSpec(memory_space=pl.ANY)],
        out_specs=[vmem] * 2,
        out_shape=[
            jax.ShapeDtypeStruct((rows, width), value.dtype),
            jax.ShapeDtypeStruct((total - rows, width), value.dtype),
        ],
        cost_estimate=pl.CostEstimate(flops=0, bytes_accessed=4 * value.size, transcendentals=0),
        name="split_rows",
    )(value, after)


def source_of(place_ref, i, peers):
    chips = peers // 2
    core = place_ref[1] if i < chips else 1 - place_ref[1]
    return lax.rem(place_ref[0] + chips - i % chips, chips) * 2 + core


def token_kernel(
    place_ref, mid_ref, count_row_ref, count_col_ref, pool_ref, gain_ref, *refs, head_dim, parts,
):
    qkv_ref, gate_ref, single_ref, normed_ref, w_ref, sems = refs[-6:]
    loads = []
    for i, (slot, row, rows) in enumerate(parts):
        dst = w_ref.at[slot, pl.ds(row, rows)]
        loads.append(pltpu.make_async_copy(refs[i], dst, sems.at[i]))
    for load in loads:
        load.start()
    peers, samples, atoms, channels = mid_ref.shape
    toks = count_col_ref.shape[0]
    total = peers * atoms
    counts = count_col_ref[...]
    row = lax.broadcasted_iota(jnp.int32, (toks, toks), 0)
    col = lax.broadcasted_iota(jnp.int32, (toks, toks), 1)
    spread = jnp.broadcast_to(count_row_ref[...], (toks, toks))
    ends = jnp.sum(jnp.where(col <= row, spread, 0.0), axis=1, keepdims=True)
    begins = ends - counts
    atom = lax.broadcasted_iota(jnp.int32, (toks, total), 1).astype(F32)
    onehot = jnp.where((atom >= begins) & (atom < ends), 1.0, 0.0).astype(BF)
    for s in range(samples):
        mid = mid_ref[:, s].reshape(total, channels)
        lifted = jnp.dot(mid, pool_ref[...], preferred_element_type=F32)
        lifted = jnp.maximum(lifted, 0.0).astype(BF)
        single = jnp.dot(onehot, lifted, preferred_element_type=F32) / counts
        single_ref[s] = single
        normed_ref[s * toks : (s + 1) * toks, :] = layer_norm(single, gain_ref[...]).astype(BF)

    for load in loads:
        load.wait()
    scale = LOG2E / float(np.sqrt(head_dim))
    width = w_ref.shape[1] // 4
    local = width // head_dim
    for i in range(peers):
        p = source_of(place_ref, i, peers)
        turned = dot(w_ref[i], normed_ref[...], (1, 1))
        for hh in range(local):
            for s in range(samples):
                for f in range(4):
                    lo = f * width + hh * head_dim
                    tile = turned[lo : lo + head_dim, s * toks : (s + 1) * toks]
                    if f == 0:
                        tile = tile * scale
                    if f < 3:
                        qkv_ref[p * local + hh, s, f] = tile.astype(BF)
                    else:
                        gate_ref[p * local + hh, s] = tile.astype(BF)


def pool_and_project(place, mid, count, pool, gain, pieces, heads, others):
    peers, samples, atoms, channels = mid.shape
    toks = count.shape[0]
    width = pool.shape[1]
    head_dim = width // heads
    count = count.astype(F32)
    row, col = count.reshape(1, toks), count.reshape(toks, 1)
    gain = gain.reshape(1, width)
    vmem = pl.BlockSpec(memory_space=pltpu.VMEM)
    hbm = pl.BlockSpec(memory_space=pl.ANY)
    parts = tuple((slot, first, array.shape[0]) for slot, first, array in pieces)
    return pl.pallas_call(
        functools.partial(token_kernel, head_dim=head_dim, parts=parts),
        in_specs=[pl.BlockSpec(memory_space=pltpu.SMEM)] + [vmem] * 5 + [hbm] * (len(pieces) + len(others)),
        out_specs=[vmem] * 3,
        out_shape=[
            jax.ShapeDtypeStruct((heads, samples, 3, head_dim, toks), BF),
            jax.ShapeDtypeStruct((heads, samples, head_dim, toks), BF),
            jax.ShapeDtypeStruct((samples, toks, width), F32),
        ],
        scratch_shapes=[
            pltpu.VMEM((samples * toks, width), BF),
            pltpu.VMEM((peers,) + pieces[0][2].shape, BF),
            pltpu.SemaphoreType.DMA((len(pieces),)),
        ],
        compiler_params=pltpu.CompilerParams(vmem_limit_bytes=VMEM_MOST),
        cost_estimate=pl.CostEstimate(flops=6_000_000_000, bytes_accessed=8_000_000, transcendentals=1000),
        name="pool_and_project",
    )(place, mid, row, col, pool, gain, *[array for _, _, array in pieces], *others)


def attend_kernel(place_ref, qkv_ref, *refs):
    out_ref, keys_ref, values_ref = refs[-3:]
    half = (len(refs) - 3) // 2
    upper, lower = refs[:half], refs[half : 2 * half]
    peers, samples, _, head_dim, toks = qkv_ref.shape
    qblocks = out_ref.shape[0]
    width = upper[0].shape[1]
    per = width // toks
    step = pl.program_id(0)
    first = pl.num_programs(0) // 2

    def load(order):
        for s in range(samples):
            for i, p in enumerate(order):
                lanes = slice(i * toks, (i + 1) * toks)
                keys_ref[s, :, lanes] = qkv_ref[p, s, 1]
                values_ref[s, :head_dim, lanes] = qkv_ref[p, s, 2]
            values_ref[s, head_dim:, :] = jnp.ones((values_ref.shape[1] - head_dim, peers * toks), BF)

    def attend(tiles):
        for s in range(samples):
            queries = jnp.concatenate(
                [qkv_ref[step * qblocks + j, s, 0] for j in range(qblocks)], axis=1
            ).T
            top = None
            for i, tile in enumerate(tiles):
                lanes = slice(i * width, (i + 1) * width)
                scores = dot(queries, keys_ref[s, :, lanes], (1, 0)) + tile[...].astype(F32)
                peak = jnp.max(scores, axis=1, keepdims=True)
                if i > 0:
                    peak = jnp.maximum(top, peak)
                weights = jnp.exp2(scores - peak).astype(BF)
                part = dot(weights, values_ref[s, :, lanes], (1, 1))
                mixed = part if i == 0 else mixed * jnp.exp2(top - peak) + part
                top = peak
            turned = (mixed / mixed[:, head_dim : head_dim + 1]).T
            for j in range(qblocks):
                out_ref[j, s] = turned[:head_dim, j * toks : (j + 1) * toks].astype(BF)

    @pl.when(step == 0)
    def _():
        sources = [source_of(place_ref, i, half) for i in range(half)]
        load([source * per + j for source in sources for j in range(per)])

    @pl.when(step < first)
    def _():
        attend(upper)

    @pl.when(step >= first)
    def _():
        attend(lower)


def token_attention(place, qkv, upper, lower):
    peers, samples, _, head_dim, toks = qkv.shape
    rows, width = upper[0].shape
    qblocks = 4
    tile = qblocks * toks
    keys = peers * toks
    first = rows // tile
    early = lambda i: (jnp.minimum(i, first - 1), 0)
    late = lambda i: (jnp.maximum(i - first, 0), 0)
    return pl.pallas_call(
        attend_kernel,
        grid=(keys // tile,),
        in_specs=[
            pl.BlockSpec(memory_space=pltpu.SMEM),
            pl.BlockSpec(qkv.shape, lambda i: (0, 0, 0, 0, 0)),
        ] + [pl.BlockSpec((tile, width), early)] * len(upper)
        + [pl.BlockSpec((tile, width), late)] * len(lower),
        out_specs=pl.BlockSpec((qblocks, samples, head_dim, toks), lambda i: (i, 0, 0, 0)),
        out_shape=jax.ShapeDtypeStruct((peers, samples, head_dim, toks), BF),
        scratch_shapes=[
            pltpu.VMEM((samples, head_dim, keys), BF),
            pltpu.VMEM((samples, head_dim + 16, keys), BF),
        ],
        compiler_params=params(VMEM_MOST),
        cost_estimate=pl.CostEstimate(
            flops=4 * samples * keys * keys * 128, bytes_accessed=2 * keys * keys + 2 * qkv.size,
            transcendentals=samples * keys * keys,
        ),
        name="token_attention",
    )(place, qkv, *upper, *lower)


def out_kernel(mixed_ref, gate_ref, single_ref, out_proj_ref, return_ref, back_ref):
    heads, samples, head_dim, toks = mixed_ref.shape
    for s in range(samples):
        gate = jax.nn.sigmoid(gate_ref[:, s].astype(F32))
        gated = (gate * mixed_ref[:, s].astype(F32)).astype(BF).reshape(heads * head_dim, toks)
        new = single_ref[s] + dot(gated, out_proj_ref[...], (0, 0))
        back_ref[s] = jnp.dot(new.astype(BF), return_ref[...], preferred_element_type=F32).astype(BF)


def out_project(mixed, gate, single, out_proj, return_proj):
    return pl.pallas_call(
        out_kernel,
        out_shape=jax.ShapeDtypeStruct(single.shape[:2] + return_proj.shape[1:], BF),
        compiler_params=pltpu.CompilerParams(vmem_limit_bytes=VMEM_LIMIT),
        cost_estimate=pl.CostEstimate(flops=400_000_000, bytes_accessed=4_000_000, transcendentals=200_000),
        name="out_project",
    )(mixed, gate, single, out_proj, return_proj)


def spread_kernel(tok_ref, back_ref, mid_ref, out_ref):
    samples, atoms, channels = mid_ref.shape
    toks = back_ref.shape[1]
    col = lax.broadcasted_iota(jnp.int32, (atoms, toks), 1)
    onehot = jnp.where(col == tok_ref[...], 1.0, 0.0).astype(BF)
    for s in range(samples):
        spread = jnp.dot(onehot, back_ref[s], preferred_element_type=F32)
        out_ref[s] = (mid_ref[s].astype(F32) + spread).astype(BF)


def spread_back(local_tok, back, mid):
    return pl.pallas_call(
        spread_kernel,
        out_shape=jax.ShapeDtypeStruct(mid.shape, BF),
        compiler_params=pltpu.CompilerParams(vmem_limit_bytes=VMEM_LIMIT),
        cost_estimate=pl.CostEstimate(flops=100_000_000, bytes_accessed=2_000_000, transcendentals=0),
        name="spread_back",
    )(local_tok, back, mid)


def shards(
    atom_feats, atom_pair, key_shift, atom_token, token_count, atom_gain, atom_qkv,
    atom_out_proj, atom_pair_proj, pool_proj, token_gain, token_qkvg, pair_tiles, pair_proj,
    token_out_proj, return_proj,
):
    samples, atoms, channels = atom_feats.shape
    toks = token_count.shape[0]
    width = token_qkvg.shape[0]
    heads = pair_proj.shape[1]
    peers = lax.axis_size("col")
    seqs = lax.axis_size("seq")
    devices = peers * seqs
    qblock, window = atom_pair.shape[2:]
    margin = window // 2 - qblock // 2 + qblock

    up = [(i, i + 1) for i in range(devices - 1)]
    down = [(j, i) for i, j in up]
    before = lax.ppermute(atom_feats, ("seq", "col"), up)
    after = lax.ppermute(atom_feats, ("seq", "col"), down)

    chips = peers // 2
    col = lax.axis_index("col")
    place = jnp.stack([col // 2, col % 2]).astype(jnp.int32)

    def along(value, hop):
        pairs = [(2 * x + k, 2 * ((x + hop) % chips) + k) for x in range(chips) for k in range(2)]
        return lax.ppermute(value, "col", pairs)

    def across(value):
        return lax.ppermute(value, "col", [(i, i ^ 1) for i in range(peers)])

    own_w = jnp.transpose(token_qkvg, (1, 2, 0)).reshape(-1, width)
    back_w, ahead_w = along(own_w, 1), along(own_w, -1)

    tile_bias = jnp.einsum("ijc,ch->hij", pair_tiles, pair_proj, preferred_element_type=F32)
    tile_bias = (tile_bias * LOG2E).astype(BF)
    head_bias = lax.all_to_all(tile_bias, "seq", split_axis=0, concat_axis=0, tiled=True)

    index = lax.axis_index(("seq", "col"))
    offset = (index * atoms).astype(jnp.int32).reshape(1)
    mid, done = atom_attention(
        atom_feats, before, after, atom_pair, key_shift, offset, atoms * devices,
        atom_gain.reshape(1, -1), atom_qkv, atom_out_proj, atom_pair_proj.astype(F32),
        (back_w, ahead_w),
    )
    mine = lax.all_to_all(
        mid.reshape(peers, samples // peers, atoms, channels), "col", split_axis=0, concat_axis=0, tiled=True
    )
    half = seqs * toks // 2
    upper, lower = split_rows(head_bias.reshape(seqs * toks, -1), half, done)
    pieces = [(0, 0, own_w), (1, 0, back_w), (2, 0, tie(along(own_w, 2), upper)), (3, 0, ahead_w)]
    pieces += [(slot + chips, first, across(array)) for slot, first, array in pieces]
    back_upper, ahead_lower = along(upper, 1), along(lower, -1)
    qkv, gate, single = pool_and_project(
        place, mine, token_count, pool_proj, token_gain, pieces, heads, (ahead_lower,)
    )
    back_lower, ahead_upper = along(lower, 1), along(upper, -1)
    uppers = [upper, back_upper, along(back_upper, 1), ahead_upper]
    lowers = [lower, back_lower, along(ahead_lower, -1), ahead_lower]
    qkv = lax.all_to_all(qkv, "seq", split_axis=0, concat_axis=0, tiled=True)
    uppers += [across(piece) for piece in uppers]
    lowers += [across(piece) for piece in lowers]
    mixed = token_attention(place, qkv, uppers, lowers)
    mixed = lax.all_to_all(mixed, "seq", split_axis=0, concat_axis=0, tiled=True)
    back = out_project(mixed, gate, single, token_out_proj, return_proj)
    back = lax.all_gather(back, "col", axis=0, tiled=True)
    local_tok = (atom_token - lax.axis_index("seq") * toks).reshape(atoms, 1)
    return spread_back(local_tok, back, mid)


def solution(mesh):
    placed = (
        P(None, ("seq", "col"), None),
        P(None, ("seq", "col"), None, None),
        P(("seq", "col")),
        P(("seq", "col")),
        P("seq"),
        P(),
        P(),
        P(),
        P(),
        P(),
        P(),
        P(None, None, "col"),
        P("seq", "col", None),
        P(),
        P(),
        P(),
    )
    return jax.shard_map(
        shards, mesh=mesh, in_specs=placed, out_specs=P(None, ("seq", "col"), None), check_vma=False
    )
```
